256 devices in a mesh: dp: 32 (over z, x), expert: 8 (over y, core).
Axes of the slice: x: 4, y: 4, z: 8, core: 2. Of those that a mesh axis runs over, the one named last changes fastest.
Arguments:
- out_grad: bfloat16 [1024, 3072], P('expert'), may hold values from -1.1953125 to 1.1953125
- routes: int32 [1024, 4], P('expert'), may hold values from 0 to 7, all different within a row; in each aligned block of 128 rows (0 to 127, 128 to 255, ...) at most 80 rows name the same one
- gate_values: float32 [1024, 4], P('expert'), may hold values from 0.1 to 0.5
- layer_input: bfloat16 [1024, 3072], P('expert'), may hold values from -6 to 6
- w_gate: bfloat16 [8, 3072, 8192], P('expert', None, 'dp'), may hold values from -0.109375 to 0.109375
- w_up: bfloat16 [8, 3072, 8192], P('expert', None, 'dp'), may hold values from -0.109375 to 0.109375
- w_down: bfloat16 [8, 3072, 8192], P('expert', None, 'dp'), may hold values from -0.109375 to 0.109375
Outputs:
- input_grad: bfloat16 [1024, 3072], P('expert')
- grad_gate: float32 [8, 3072, 8192], P('expert', None, 'dp')
- grad_up: float32 [8, 3072, 8192], P('expert', None, 'dp')
The draws below stay inside these ranges and needn't reach their ends.
Inputs may be any that keep to these rules, and one draw needn't show every extreme that they name: In every aligned block of 128 tokens (the tokens of one index of expert) no expert is named by more than 80 routes, a bound that some block reaches; the 4 experts of a token differ.
All inputs are finite; a program needn't handle non-finite values.
Results may differ from the reference program's by a relative error of at most 0.024.
Values may be sent and summed in bfloat16 or wider, within the bound.
A program may use at most 128 MiB of HBM per device.

```python
import math
import jax
import jax.numpy as jnp
import numpy as np
from jax import lax

D = 3072
TOP = 4
FW = 8192
EXPERTS = 8
TOK_DEV = 128
MOST = 80
TOKENS = 1024
N_DP = 32
N_EXPERT = 8


def block_scale(key, shape, pieces, least, largest):
    def one(position, parts):
        steps = jax.random.uniform(jax.random.fold_in(jax.random.fold_in(key, 6), position), (parts,), jnp.float32, least / len(pieces), largest / len(pieces))
        return jnp.repeat(jnp.exp(steps), shape[position] // parts).reshape((-1,) + (1,) * (len(shape) - position - 1))

    level = one(*pieces[0])
    for cut in pieces[1:]:
        level = level * one(*cut)
    return level


def assign_block(stream_key, own, number, rows, amount, top, reach, skew):
    order = jax.random.permutation(stream_key, amount)
    packed, usual = load_shares(amount, rows * top, reach, skew, True), load_shares(amount, rows * top, reach, skew, False)
    places = jnp.arange(amount)

    def named(lengths, rotation):
        used = int((lengths > 0).sum())
        fixed = max(1, used // 4)
        passed = fixed + (places - fixed + rotation * (used - fixed)) % max(1, amount - fixed)
        return jnp.zeros((amount,), jnp.int32).at[order[jnp.where(places < fixed, places, passed)]].set(jnp.asarray(lengths, jnp.int32))

    lengths = jnp.where(number % 4 == 0, named(packed, number // 4), named(usual, number - number // 4 - 1))
    mixed = jax.random.permutation(jax.random.fold_in(own, 3), amount)
    source_of, sink = mixed[0:amount // 2 * 2:2], mixed[1:amount // 2 * 2:2]
    slack = jnp.minimum(lengths[source_of] - 1, reach - lengths[sink]) // 2
    slack = jnp.where((source_of == order[0]) | (sink == order[0]) | (lengths[sink] == 0), 0, jnp.maximum(slack, 0))
    passed = jax.random.randint(jax.random.fold_in(own, 4), (amount // 2,), 0, 1 << 20) % (slack + 1)
    lengths = lengths.at[source_of].add(-passed).at[sink].add(passed)
    items = jnp.searchsorted(jnp.cumsum(lengths), jnp.arange(rows * top), side="right").astype(jnp.int32)
    grid = items.reshape(top, rows).T
    grid = grid[jax.random.permutation(jax.random.fold_in(own, 1), rows)]
    rotation = jax.random.randint(jax.random.fold_in(own, 2), (rows, 1), 0, top)
    return jnp.take_along_axis(grid, (jnp.arange(top)[None, :] + rotation) % top, axis=1)


def load_shares(number_of, total, bound, slope, full):
    weights = [(1 << 20) // math.isqrt(rank ** slope) + 1 for rank in range(1, number_of + 1)]
    largest = bound if full else min(bound, max(-(-total // number_of), total * weights[0] // sum(weights)))
    least = 1 if total - largest >= number_of - 1 else 0
    given, surplus = [largest] + [least] * (number_of - 1), total - largest - least * (number_of - 1)
    while surplus > 0:
        free = [i for i in range(1, number_of) if given[i] < largest] or [i for i in range(1, number_of) if given[i] < bound]
        pool, left = sum([weights[i] for i in free]), surplus
        for i in free:
            addition = min(bound - given[i], max(1, left * weights[i] // pool), surplus)
            given[i] = given[i] + addition
            surplus = surplus - addition
    return np.array(given)


def scatter_about(rng, dims, spread, bound, shards=(), kind=jnp.bfloat16):
    result = jax.random.normal(rng, dims, jnp.float32) * spread
    if len(shards) > 0:
        result = block_scale(rng, dims, shards, -0.22, 0.18) * result
    return jnp.clip(result, min=-bound, max=bound).astype(kind)


def setup_inputs(seed: int = 0) -> dict:
    keys = jax.random.split(jax.random.key(seed), 8)
    out_grad = scatter_about(keys[0], (TOKENS, D), 0.2, 1.1953125, ((0, 8),))
    routes_keys = jax.random.split(jax.random.fold_in(keys[1], 1), TOKENS // TOK_DEV)
    routes_turns = jax.random.permutation(jax.random.fold_in(keys[1], 3), TOKENS // TOK_DEV)
    routes = jax.vmap(lambda own, number: assign_block(jax.random.fold_in(keys[1], 2), own, number, TOK_DEV, EXPERTS, TOP, MOST, 1))(routes_keys, routes_turns).reshape((TOKENS, TOP))
    gate_values = jnp.clip(0.1 + 0.4 * jax.random.uniform(keys[2], (TOKENS, TOP), jnp.float32) ** block_scale(keys[2], (TOKENS, TOP), ((0, 8),), -0.2, 0.2), 0.1, 0.5)
    layer_input = scatter_about(keys[3], (TOKENS, D), 1.0, 6.0, ((0, 8),))
    w_gate = scatter_about(keys[4], (EXPERTS, D, FW), D ** -0.5, 0.109375, ((0, 8), (2, 32)))
    w_up = scatter_about(keys[5], (EXPERTS, D, FW), D ** -0.5, 0.109375, ((0, 8), (2, 32)))
    w_down = scatter_about(keys[6], (EXPERTS, D, FW), D ** -0.5, 0.109375, ((0, 8), (2, 32)))
    return dict(out_grad=out_grad, routes=routes, gate_values=gate_values, layer_input=layer_input, w_gate=w_gate, w_up=w_up, w_down=w_down)


def slot_numbers(block_routes):
    experts_row = jnp.arange(EXPERTS, dtype=jnp.int32)[None, :]
    onehot = (block_routes[:, None] == experts_row).astype(jnp.int32)
    earlier = jnp.cumsum(onehot, axis=0) - onehot
    return jnp.sum(earlier * onehot, axis=1).astype(jnp.int32)


def one_expert(inputs_one):
    rows_in, grads_in, weight_gate, weight_up, weight_down = inputs_one
    highest = lax.Precision.HIGHEST
    rows_float = rows_in.reshape(-1, D).astype(jnp.float32)
    grads_float = grads_in.reshape(-1, D).astype(jnp.float32)
    gate_float = weight_gate.astype(jnp.float32)
    up_float = weight_up.astype(jnp.float32)
    down_float = weight_down.astype(jnp.float32)
    gate_pre = jnp.dot(rows_float, gate_float, precision=highest, preferred_element_type=jnp.float32)
    up_pre = jnp.dot(rows_float, up_float, precision=highest, preferred_element_type=jnp.float32)
    sigmoid_gate = jax.nn.sigmoid(gate_pre)
    activated = gate_pre * sigmoid_gate
    hidden_grad = jnp.dot(grads_float, down_float, precision=highest, preferred_element_type=jnp.float32)
    up_grad = (hidden_grad * activated).astype(jnp.bfloat16)
    gate_grad = (hidden_grad * up_pre * sigmoid_gate * (1.0 + gate_pre * (1.0 - sigmoid_gate))).astype(jnp.bfloat16)
    gate_grad_float = gate_grad.astype(jnp.float32)
    up_grad_float = up_grad.astype(jnp.float32)
    units = FW // N_DP

    def group_term(group, total):
        first = (group * units).astype(jnp.int32)
        part_gate = lax.dynamic_slice_in_dim(gate_grad_float, first, units, 1)
        part_up = lax.dynamic_slice_in_dim(up_grad_float, first, units, 1)
        cols_gate = lax.dynamic_slice_in_dim(gate_float, first, units, 1)
        cols_up = lax.dynamic_slice_in_dim(up_float, first, units, 1)
        partial_value = jnp.dot(part_gate, cols_gate.T, precision=highest, preferred_element_type=jnp.float32)
        partial_value = partial_value + jnp.dot(part_up, cols_up.T, precision=highest, preferred_element_type=jnp.float32)
        rounded = lax.optimization_barrier(partial_value.astype(jnp.bfloat16))
        return total + rounded.astype(jnp.float32)

    start_total = jnp.zeros((rows_float.shape[0], D), jnp.float32)
    route_sum = lax.fori_loop(jnp.int32(0), jnp.int32(N_DP), group_term, start_total)
    route_sum = route_sum.astype(jnp.bfloat16).reshape(N_EXPERT, MOST, D)
    term_gate = jnp.dot(rows_float.T, gate_grad_float, precision=highest, preferred_element_type=jnp.float32)
    term_up = jnp.dot(rows_float.T, up_grad_float, precision=highest, preferred_element_type=jnp.float32)
    return route_sum, term_gate, term_up


def reference(out_grad, routes, gate_values, layer_input, w_gate, w_up, w_down):
    blocks = N_EXPERT
    flat_routes = routes.reshape(blocks, TOK_DEV * TOP)
    slot_index = jax.vmap(slot_numbers)(flat_routes)
    target = (flat_routes * MOST + slot_index).astype(jnp.int32)
    scaled = gate_values.reshape(blocks, TOK_DEV, TOP, 1) * out_grad.reshape(blocks, TOK_DEV, 1, D).astype(jnp.float32)
    scaled = scaled.reshape(blocks, TOK_DEV * TOP, D).astype(jnp.bfloat16)
    copies = jnp.broadcast_to(layer_input.reshape(blocks, TOK_DEV, 1, D), (blocks, TOK_DEV, TOP, D))
    copies = copies.reshape(blocks, TOK_DEV * TOP, D)
    block_index = jnp.broadcast_to(jnp.arange(blocks, dtype=jnp.int32)[:, None], target.shape)
    blank_slots = jnp.zeros((blocks, EXPERTS * MOST, D), jnp.bfloat16)
    sent_grads = blank_slots.at[block_index, target].set(scaled)
    sent_grads = sent_grads.reshape(blocks, EXPERTS, MOST, D).transpose(1, 0, 2, 3)
    sent_rows = blank_slots.at[block_index, target].set(copies)
    sent_rows = sent_rows.reshape(blocks, EXPERTS, MOST, D).transpose(1, 0, 2, 3)
    route_all, grad_gate, grad_up = lax.map(one_expert, (sent_rows, sent_grads, w_gate, w_up, w_down))
    returned = route_all.transpose(1, 0, 2, 3).reshape(blocks, EXPERTS * MOST, D)
    picked = jnp.take_along_axis(returned, target[:, :, None], axis=1).astype(jnp.float32)
    input_grad = jnp.sum(picked.reshape(TOKENS, TOP, D), axis=1).astype(jnp.bfloat16)
    return input_grad, grad_gate, grad_up
```

```python
import jax
import jax.numpy as jnp
from jax import lax
from jax.sharding import PartitionSpec as P

EXPERTS = 8


def local(out_grad, routes, gate_values, layer_input, w_gate, w_up, w_down):
    me = lax.axis_index("expert")
    w_gate, w_up, w_down = w_gate[0], w_up[0], w_down[0]
    experts_row = jnp.arange(EXPERTS, dtype=jnp.int32)
    dense = jnp.sum(
        jnp.where(routes[:, :, None] == experts_row, gate_values[:, :, None], 0.0), axis=1
    )
    weight = lax.all_gather(dense, "expert", axis=0, tiled=True)
    weight = lax.dynamic_slice_in_dim(weight, me, 1, axis=1)
    rows = lax.all_gather(layer_input, "expert", axis=0, tiled=True)
    grads = lax.all_gather(out_grad, "expert", axis=0, tiled=True)
    gate_pre = jnp.dot(rows, w_gate, preferred_element_type=jnp.float32)
    up_pre = jnp.dot(rows, w_up, preferred_element_type=jnp.float32)
    hidden_grad = weight * jnp.dot(grads, w_down, preferred_element_type=jnp.float32)
    sigmoid_gate = jax.nn.sigmoid(gate_pre)
    activated = gate_pre * sigmoid_gate
    up_grad = (hidden_grad * activated).astype(jnp.bfloat16)
    gate_grad = (
        hidden_grad * up_pre * sigmoid_gate * (1.0 + gate_pre * (1.0 - sigmoid_gate))
    ).astype(jnp.bfloat16)
    partial = jnp.dot(gate_grad, w_gate.T, preferred_element_type=jnp.float32)
    partial = partial + jnp.dot(up_grad, w_up.T, preferred_element_type=jnp.float32)
    total = lax.psum_scatter(partial.astype(jnp.bfloat16), "expert", scatter_dimension=0, tiled=True)
    total = lax.psum(total, "dp")
    grad_gate = jnp.dot(rows.T, gate_grad, preferred_element_type=jnp.float32)
    grad_up = jnp.dot(rows.T, up_grad, preferred_element_type=jnp.float32)
    return total, grad_gate[None], grad_up[None]


def solution(mesh):
    placed = (
        P("expert", None),
        P("expert", None),
        P("expert", None),
        P("expert", None),
        P("expert", None, "dp"),
        P("expert", None, "dp"),
        P("expert", None, "dp"),
    )
    return jax.shard_map(
        local,
        mesh=mesh,
        in_specs=placed,
        out_specs=(P("expert", None), P("expert", None, "dp"), P("expert", None, "dp")),
        check_vma=False,
    )
```

```python
import functools

import jax
import jax.numpy as jnp
from jax import lax
from jax.experimental import pallas as pl
from jax.experimental.pallas import tpu as pltpu
from jax.sharding import PartitionSpec as P

MESH = pl.DeviceIdType.MESH
BF16, F32 = jnp.bfloat16, jnp.float32
EXPERTS = 8
NX, NY, NZ = 4, 4, 8
TOK, D, U = 128, 3072, 256
HALF = TOK // 2
XROWS = HALF // NX
ZCOLS = D // NZ
OWN, UP, DOWN, FAR = 0, 1, 2, 3
TILE = 256


def kernel(
    og_in, routes_in, gates_in, x_in, wg_in, wu_in, wd_in,
    out_hbm, gg_hbm, gu_hbm,
    xo, wgu, wd, g8, dg, ps, pr, s, xr, u, zr, v, yr, out, grads,
    load_sem, send_sem, recv_sem, grad_sem,
):
    dp, ex = lax.axis_index("dp"), lax.axis_index("expert")
    x, z = lax.rem(dp, NX), lax.div(dp, NX)
    y, c = lax.div(ex, 2), lax.rem(ex, 2)

    def dev(nx, ny, nz, nc):
        return (nz * NX + nx, ny * 2 + nc)

    sib = dev(x, y, z, 1 - c)
    y_at = {d: lax.rem(y + d, NY) for d in (1, 2, 3)}
    x_at = {d: lax.rem(x + d, NX) for d in (1, 2, 3)}
    z_at = {d: lax.rem(z + d, NZ) for d in range(1, NZ)}
    to_y = {d: dev(x, y_at[d], z, c) for d in y_at}
    to_x = {d: dev(x_at[d], y, z, c) for d in x_at}
    to_z = {d: dev(x, y, z_at[d], c) for d in z_at}

    loads = []

    def load(src, dst):
        copy = pltpu.make_async_copy(src, dst, load_sem.at[len(loads)])
        copy.start()
        loads.append(copy)
        return copy

    sent = []

    def send(src, dst, device):
        i = len(sent)
        copy = pltpu.make_async_remote_copy(
            src_ref=src, dst_ref=dst, send_sem=send_sem.at[i], recv_sem=recv_sem.at[i],
            device_id=device, device_id_type=MESH,
        )
        copy.start()
        sent.append(copy)
        return copy

    own_loads = {}
    for h in range(2):
        for a, ref in ((0, x_in), (1, og_in)):
            own_loads[a, h] = load(ref.at[pl.ds(h * HALF, HALF)], xo.at[a, h, OWN, 0])
    weight_loads = [
        load(wg_in.at[0], wgu.at[:, pl.ds(0, U)]),
        load(wu_in.at[0], wgu.at[:, pl.ds(U, U)]),
        load(wd_in.at[0], wd),
    ]

    peers = [sib] + list(to_y.values()) + list(to_x.values()) + list(to_z.values())
    barrier = pltpu.get_barrier_semaphore()
    for device in peers:
        pl.semaphore_signal(barrier, inc=1, device_id=device, device_id_type=MESH)

    lane = lax.broadcasted_iota(jnp.int32, (TOK, TOK), 1)
    row = lax.broadcasted_iota(jnp.int32, (TOK, TOK), 0)
    for e in range(EXPERTS):
        column = jnp.sum(jnp.where(routes_in[...] == e, gates_in[...], 0.0), axis=1, keepdims=True)
        g8[OWN, 0, e : e + 1, :] = jnp.sum(jnp.where(lane == row, column, 0.0), axis=0, keepdims=True)

    pl.semaphore_wait(barrier, len(peers))

    g_move = {
        DOWN: send(g8.at[OWN, 0], g8.at[DOWN, 0], to_y[1]),
        UP: send(g8.at[OWN, 0], g8.at[UP, 0], to_y[3]),
        FAR: send(g8.at[OWN, 0], g8.at[FAR, 0], to_y[2]),
    }
    g_swap = {OWN: send(g8.at[OWN, 0], g8.at[OWN, 1], sib)}
    move, swap = {}, {}

    def send_own(h):
        for a in (0, 1):
            move[a, h, DOWN] = send(xo.at[a, h, OWN, 0], xo.at[a, h, DOWN, 0], to_y[1])
            b = 1 - a
            move[b, h, UP] = send(xo.at[b, h, OWN, 0], xo.at[b, h, UP, 0], to_y[3])

    def do_swap(a, h, j):
        swap[a, h, j] = send(xo.at[a, h, j, 0], xo.at[a, h, j, 1], sib)

    for a in range(2):
        own_loads[a, 0].wait()
    send_own(0)
    for h in range(2):
        for a in range(2):
            if h:
                own_loads[a, h].wait()
            do_swap(a, h, OWN)

    def first_pieces(h):
        move[0, h, DOWN].wait_recv()
        move[0, h, FAR] = send(xo.at[0, h, DOWN, 0], xo.at[0, h, FAR, 0], to_y[1])
        move[1, h, UP].wait_recv()
        move[1, h, FAR] = send(xo.at[1, h, UP, 0], xo.at[1, h, FAR, 0], to_y[3])
        do_swap(0, h, DOWN)
        do_swap(1, h, UP)

    def second_pieces(h):
        move[1, h, DOWN].wait_recv()
        do_swap(1, h, DOWN)
        move[0, h, UP].wait_recv()
        do_swap(0, h, UP)

    def far_pieces(h):
        for a in range(2):
            move[a, h, FAR].wait_recv()
            do_swap(a, h, FAR)

    def weight_column(h, j, slot):
        mine = lax.broadcasted_iota(jnp.int32, (EXPERTS, TOK), 0) == ex
        line = jnp.sum(jnp.where(mine, g8[j, slot], 0.0), axis=0, keepdims=True)
        whole = jnp.sum(jnp.where(lane == row, line, 0.0), axis=1, keepdims=True)
        return whole[h * HALF : (h + 1) * HALF]

    def compute(h, j, n):
        rows = n * TOK
        for jj in range(j, j + n):
            for a in range(2):
                swap[a, h, jj].wait_recv()
        weight = jnp.concatenate(
            [weight_column(h, jj, slot) for jj in range(j, j + n) for slot in range(2)], axis=0
        )
        tokens = xo[0, h, j : j + n].reshape(rows, D)
        gate_pre = jnp.dot(tokens, wgu[:, :U], preferred_element_type=F32)
        up_pre = jnp.dot(tokens, wgu[:, U:], preferred_element_type=F32)
        grads_in = xo[1, h, j : j + n].reshape(rows, D)
        hidden = weight * jnp.dot(grads_in, wd[...], preferred_element_type=F32)
        sig = jax.nn.sigmoid(gate_pre)
        up_grad = (hidden * (gate_pre * sig)).astype(BF16)
        gate_grad = (hidden * up_pre * sig * (1.0 + gate_pre * (1.0 - sig))).astype(BF16)
        both = jnp.concatenate([gate_grad, up_grad], axis=1)
        dg[h, j : j + n] = both.reshape(n, 2, HALF, 2 * U)

        def tile(i, carry):
            cols = pl.ds(pl.multiple_of(i * TILE, TILE), TILE)
            part = lax.dot_general(
                dg[h, j : j + n].reshape(rows, 2 * U), wgu[cols, :], (((1,), (1,)), ((), ())),
                preferred_element_type=F32,
            ).astype(BF16).reshape(n, 2, HALF, TILE)
            s[h, j : j + n, :, cols] = part[:, 0]
            ps[h, j : j + n, :, cols] = part[:, 1]
            return carry

        lax.fori_loop(0, D // TILE, tile, 0)

    def swap_parts(h, j, n):
        return send(ps.at[h, pl.ds(j, n)], pr.at[h, pl.ds(j, n)], sib)

    def scatter_x(h, j, n, swapped):
        swapped.wait_recv()
        for jj in range(j, j + n):
            s[h, jj] = (s[h, jj].astype(F32) + pr[h, jj].astype(F32)).astype(BF16)
        got = []
        for d in (1, 3, 2):
            rows = pl.ds(pl.multiple_of(x_at[d] * XROWS, XROWS), XROWS)
            got.append(
                send(s.at[h, pl.ds(j, n), rows], xr.at[d - 1, h, pl.ds(j, n)], to_x[d])
            )
        return got

    def sum_x(h, j, n, got):
        for copy in got:
            copy.wait_recv()
        rows = pl.ds(pl.multiple_of(x * XROWS, XROWS), XROWS)
        for jj in range(j, j + n):
            total = s[h, jj, rows].astype(F32)
            for d in range(3):
                total = total + xr[d, h, jj].astype(F32)
            u[h, jj] = total.astype(BF16)

    def scatter_z(h, j, n):
        got = []
        for d in (1, 7, 2, 6, 3, 5, 4):
            cols = pl.ds(pl.multiple_of(z_at[d] * ZCOLS, ZCOLS), ZCOLS)
            got.append(
                send(u.at[h, pl.ds(j, n), :, cols], zr.at[d - 1, h, pl.ds(j, n)], to_z[d])
            )
        return got

    my_cols = pl.ds(pl.multiple_of(z * ZCOLS, ZCOLS), ZCOLS)

    def sum_z(h, j, n, got):
        for copy in got:
            copy.wait_recv()
        for jj in range(j, j + n):
            total = u[h, jj, :, my_cols].astype(F32)
            for d in range(NZ - 1):
                total = total + zr[d, h, jj].astype(F32)
            v[h, jj] = total.astype(BF16)

    def scatter_y(h):
        return [
            send(v.at[h, j], yr.at[h, j - 1], to_y[d])
            for j, d in ((UP, 1), (DOWN, 3), (FAR, 2))
        ]

    def place(h):
        return pl.ds(pl.multiple_of(h * HALF + x * XROWS, XROWS), XROWS)

    def gather_z(h, got):
        for copy in got:
            copy.wait_recv()
        total = v[h, OWN].astype(F32)
        for j in range(3):
            total = total + yr[h, j].astype(F32)
        out[place(h), my_cols] = total.astype(BF16)
        piece = out.at[place(h), my_cols]
        return [send(piece, piece, to_z[d]) for d in (1, 7, 2, 6, 3, 5, 4)]

    def gather_x(h, got):
        for copy in got:
            copy.wait_recv()
        piece = out.at[place(h)]
        return [send(piece, piece, to_x[d]) for d in (1, 3, 2)]

    grad_copies = []

    def grad_tiles(first, last):
        def tile(i, carry):
            cols = pl.ds(pl.multiple_of(i * TILE, TILE), TILE)
            part = lax.dot_general(
                xo[0, :, :, :, :, cols].reshape(8 * TOK, TILE),
                dg[...].reshape(8 * TOK, 2 * U),
                (((0,), (0,)), ((), ())),
                preferred_element_type=F32,
            )
            grads[0, cols] = part[:, :U]
            grads[1, cols] = part[:, U:]
            return carry

        lax.fori_loop(first, last, tile, 0)
        rows = pl.ds(first * TILE, (last - first) * TILE)
        for k, ref in enumerate((gg_hbm, gu_hbm)):
            copy = pltpu.make_async_copy(
                grads.at[k, rows], ref.at[0, rows], grad_sem.at[len(grad_copies)]
            )
            copy.start()
            grad_copies.append(copy)

    g_swap[OWN].wait_recv()
    for copy in weight_loads:
        copy.wait()
    compute(0, OWN, 1)
    p_own0 = swap_parts(0, OWN, 1)
    compute(1, OWN, 1)
    p_own1 = swap_parts(1, OWN, 1)
    for j in (UP, DOWN, FAR):
        g_move[j].wait_recv()
        g_swap[j] = send(g8.at[j, 0], g8.at[j, 1], sib)
    first_pieces(0)
    send_own(1)
    x_own0 = scatter_x(0, OWN, 1, p_own0)
    x_own1 = scatter_x(1, OWN, 1, p_own1)
    for j in (UP, DOWN, FAR):
        g_swap[j].wait_recv()
    second_pieces(0)
    compute(0, UP, 2)
    p_mid0 = swap_parts(0, UP, 2)
    sum_x(0, OWN, 1, x_own0)
    x_mid0 = scatter_x(0, UP, 2, p_mid0)
    sum_x(1, OWN, 1, x_own1)
    far_pieces(0)
    compute(0, FAR, 1)
    p_far0 = swap_parts(0, FAR, 1)
    sum_x(0, UP, 2, x_mid0)
    z_mid0 = scatter_z(0, OWN, 3)
    x_far0 = scatter_x(0, FAR, 1, p_far0)
    first_pieces(1)
    sum_x(0, FAR, 1, x_far0)
    z_far0 = scatter_z(0, FAR, 1)
    sum_z(0, OWN, 3, z_mid0)
    sum_z(0, FAR, 1, z_far0)
    y_0 = scatter_y(0)
    second_pieces(1)
    compute(1, UP, 2)
    p_mid1 = swap_parts(1, UP, 2)
    zg_0 = gather_z(0, y_0)
    x_mid1 = scatter_x(1, UP, 2, p_mid1)
    xg_0 = gather_x(0, zg_0)
    far_pieces(1)
    compute(1, FAR, 1)
    p_far1 = swap_parts(1, FAR, 1)
    sum_x(1, UP, 2, x_mid1)
    z_mid1 = scatter_z(1, OWN, 3)
    x_far1 = scatter_x(1, FAR, 1, p_far1)
    grad_tiles(0, 4)
    sum_x(1, FAR, 1, x_far1)
    z_far1 = scatter_z(1, FAR, 1)
    grad_tiles(4, 6)
    sum_z(1, OWN, 3, z_mid1)
    sum_z(1, FAR, 1, z_far1)
    y_1 = scatter_y(1)
    grad_tiles(6, 8)
    zg_1 = gather_z(1, y_1)
    grad_tiles(8, 10)
    xg_1 = gather_x(1, zg_1)
    grad_tiles(10, 12)
    for copy in xg_0:
        copy.wait_recv()
    for copy in xg_1:
        copy.wait_recv()
    last = pltpu.make_async_copy(out, out_hbm, load_sem.at[len(loads)])
    last.start()
    for copy in sent:
        copy.wait_send()
    for copy in grad_copies:
        copy.wait()
    last.wait()


N_SEND = 128


def local(out_grad, routes, gate_values, layer_input, w_gate, w_up, w_down):
    any_spec = pl.BlockSpec(memory_space=pl.ANY)
    vmem = pl.BlockSpec(memory_space=pltpu.VMEM)
    return pl.pallas_call(
        kernel,
        out_shape=(
            jax.ShapeDtypeStruct((TOK, D), BF16),
            jax.ShapeDtypeStruct((1, D, U), F32),
            jax.ShapeDtypeStruct((1, D, U), F32),
        ),
        in_specs=[any_spec, vmem, vmem, any_spec, any_spec, any_spec, any_spec],
        out_specs=(any_spec, any_spec, any_spec),
        scratch_shapes=[
            pltpu.VMEM((2, 2, 4, 2, HALF, D), BF16),
            pltpu.VMEM((D, 2 * U), BF16),
            pltpu.VMEM((D, U), BF16),
            pltpu.VMEM((4, 2, EXPERTS, TOK), F32),
            pltpu.VMEM((2, 4, 2, HALF, 2 * U), BF16),
            pltpu.VMEM((2, 4, HALF, D), BF16),
            pltpu.VMEM((2, 4, HALF, D), BF16),
            pltpu.VMEM((2, 4, HALF, D), BF16),
            pltpu.VMEM((3, 2, 4, XROWS, D), BF16),
            pltpu.VMEM((2, 4, XROWS, D), BF16),
            pltpu.VMEM((NZ - 1, 2, 4, XROWS, ZCOLS), BF16),
            pltpu.VMEM((2, 4, XROWS, ZCOLS), BF16),
            pltpu.VMEM((2, 3, XROWS, ZCOLS), BF16),
            pltpu.VMEM((TOK, D), BF16),
            pltpu.VMEM((2, D, U), F32),
            pltpu.SemaphoreType.DMA((8,)),
            pltpu.SemaphoreType.DMA((N_SEND,)),
            pltpu.SemaphoreType.DMA((N_SEND,)),
            pltpu.SemaphoreType.DMA((12,)),
        ],
        compiler_params=pltpu.CompilerParams(
            collective_id=0, has_side_effects=True, vmem_limit_bytes=56 * 2**20
        ),
        cost_estimate=pl.CostEstimate(
            flops=7 * 2 * 1024 * D * U, bytes_accessed=14 * 2**20, transcendentals=1024 * U
        ),
    )(out_grad, routes, gate_values, layer_input, w_gate, w_up, w_down)


def solution(mesh):
    placed = (
        P("expert", None),
        P("expert", None),
        P("expert", None),
        P("expert", None),
        P("expert", None, "dp"),
        P("expert", None, "dp"),
        P("expert", None, "dp"),
    )
    return jax.shard_map(
        local,
        mesh=mesh,
        in_specs=placed,
        out_specs=(P("expert", None), P("expert", None, "dp"), P("expert", None, "dp")),
        check_vma=False,
    )
```

```python
import functools

import jax
import jax.numpy as jnp
from jax import lax
from jax.experimental import pallas as pl
from jax.experimental.pallas import tpu as pltpu
from jax.sharding import PartitionSpec as P

MESH = pl.DeviceIdType.MESH
BF16, F32 = jnp.bfloat16, jnp.float32
EXPERTS = 8
NX, NY, NZ = 4, 4, 8
TOK, D, U = 128, 3072, 256
HALF = TOK // 2
XROWS = HALF // NX
ZCOLS = D // NZ
OWN, UP, DOWN, FAR = 0, 1, 2, 3
TO_Y = ((FAR, 2), (DOWN, 1), (UP, 3))
NEAR = ((DOWN, 1), (UP, 3))
TILE = 256


def kernel(
    og_in, routes_in, gates_in, x_in, wg_in, wu_in, wd_in,
    out, gg, gu,
    xo, wgu, wd, g8, dg, ps, pr, s, xr, u, zr, v, yr,
    load_sem, send_sem, recv_sem,
):
    dp, ex = lax.axis_index("dp"), lax.axis_index("expert")
    x, z = lax.rem(dp, NX), lax.div(dp, NX)
    y, c = lax.div(ex, 2), lax.rem(ex, 2)

    def dev(nx, ny, nz, nc):
        return (nz * NX + nx, ny * 2 + nc)

    sib = dev(x, y, z, 1 - c)
    y_at = {d: lax.rem(y + d, NY) for d in (1, 2, 3)}
    x_at = {d: lax.rem(x + d, NX) for d in (1, 2, 3)}
    z_at = {d: lax.rem(z + d, NZ) for d in range(1, NZ)}
    to_y = {d: dev(x, y_at[d], z, c) for d in y_at}
    to_x = {d: dev(x_at[d], y, z, c) for d in x_at}
    to_z = {d: dev(x, y, z_at[d], c) for d in z_at}

    loads = []

    def load(src, dst):
        copy = pltpu.make_async_copy(src, dst, load_sem.at[len(loads)])
        copy.start()
        loads.append(copy)
        return copy

    sent = []

    def send(src, dst, device):
        i = len(sent)
        copy = pltpu.make_async_remote_copy(
            src_ref=src, dst_ref=dst, send_sem=send_sem.at[i], recv_sem=recv_sem.at[i],
            device_id=device, device_id_type=MESH,
        )
        copy.start()
        sent.append(copy)
        return copy

    own_loads = {}
    for h in range(2):
        for a, ref in ((0, x_in), (1, og_in)):
            own_loads[a, h] = load(ref.at[pl.ds(h * HALF, HALF)], xo.at[a, h, OWN, 0])
    weight_loads = [
        load(wg_in.at[0], wgu.at[:, pl.ds(0, U)]),
        load(wu_in.at[0], wgu.at[:, pl.ds(U, U)]),
        load(wd_in.at[0], wd),
    ]

    peers = [sib] + list(to_y.values()) + list(to_x.values()) + list(to_z.values())
    barrier = pltpu.get_barrier_semaphore()
    for device in peers:
        pl.semaphore_signal(barrier, inc=1, device_id=device, device_id_type=MESH)

    lane = lax.broadcasted_iota(jnp.int32, (TOK, TOK), 1)
    row = lax.broadcasted_iota(jnp.int32, (TOK, TOK), 0)
    for e in range(EXPERTS):
        g8[OWN, 0, e : e + 1, :] = jnp.sum(
            jnp.where(routes_in[...] == e, gates_in[...], 0.0), axis=0, keepdims=True
        )

    pl.semaphore_wait(barrier, len(peers))

    g_move = {j: send(g8.at[OWN, 0], g8.at[j, 0], to_y[d]) for j, d in TO_Y}
    g_swap = {OWN: send(g8.at[OWN, 0], g8.at[OWN, 1], sib)}
    swap = {}
    x_cols = pl.ds(pl.multiple_of(x * (D // NX), D // NX), D // NX)
    z_cols = pl.ds(pl.multiple_of(z * ZCOLS, ZCOLS), ZCOLS)

    def groups(first, count):
        return pl.ds(first * 16, count * 16)

    NEAR_D, NEAR_X, FAR_X, FAR_Z = 3, 1, 2, 2
    near_d, near_x = groups(0, NEAR_D), groups(NEAR_D, NEAR_X)
    far_x, far_z = groups(0, FAR_X), groups(FAR_X, FAR_Z)

    def move(h, j, rows, cols, device):
        piece = xo.at[:, h, OWN, 0, rows, cols]
        return send(piece, xo.at[:, h, j, 0, rows, cols], device)

    def do_swap(h, j, rows):
        swap.setdefault((h, j), []).append(send(xo.at[:, h, j, 0, rows], xo.at[:, h, j, 1, rows], sib))

    def send_small(h):
        far = [move(h, FAR, far_z, z_cols, to_y[2]), move(h, FAR, far_x, x_cols, to_y[2])]
        near = [move(h, j, near_x, x_cols, to_y[d]) for j, d in NEAR]
        return far, near

    def send_direct(h):
        return [move(h, j, near_d, slice(None), to_y[d]) for j, d in NEAR]

    def share(h, small):
        far, near = small
        for copy in far:
            copy.wait_recv()
        far_got = []
        for d in (4, 3, 5, 2, 6, 1, 7):
            piece = xo.at[:, h, FAR, 0, far_z, z_cols]
            far_got.append(send(piece, piece, to_z[d]))
        for d in (2, 1, 3):
            piece = xo.at[:, h, FAR, 0, far_x, x_cols]
            far_got.append(send(piece, piece, to_x[d]))
        for copy in near:
            copy.wait_recv()
        near_got = []
        for d in (2, 1, 3):
            piece = xo.at[:, h, pl.ds(UP, 2), 0, near_x, x_cols]
            near_got.append(send(piece, piece, to_x[d]))
        return far_got, near_got

    def far_arrive(h, got):
        for copy in got:
            copy.wait_recv()
        do_swap(h, FAR, groups(0, 4))

    def direct_arrive(h, got):
        for copy in got:
            copy.wait_recv()

    def direct_swap(h):
        for j, _ in NEAR:
            do_swap(h, j, near_d)

    def shared_arrive(h, got):
        for copy in got:
            copy.wait_recv()
        for j, _ in NEAR:
            do_swap(h, j, near_x)

    for a in range(2):
        own_loads[a, 0].wait()
    small_0 = send_small(0)
    direct_0 = send_direct(0)
    do_swap(0, OWN, groups(0, 4))
    for a in range(2):
        own_loads[a, 1].wait()
    do_swap(1, OWN, groups(0, 4))

    def weight_column(h, j, slot):
        mine = lax.broadcasted_iota(jnp.int32, (EXPERTS, TOK), 0) == ex
        line = jnp.sum(jnp.where(mine, g8[j, slot], 0.0), axis=0, keepdims=True)
        whole = jnp.sum(jnp.where(lane == row, line, 0.0), axis=1, keepdims=True)
        return whole[h * HALF : (h + 1) * HALF]

    def compute(h, j, n):
        rows = n * TOK
        for jj in range(j, j + n):
            for copy in swap[h, jj]:
                copy.wait_recv()
        weight = jnp.concatenate(
            [weight_column(h, jj, slot) for jj in range(j, j + n) for slot in range(2)], axis=0
        )
        tokens = xo[0, h, j : j + n].reshape(rows, D)
        gate_pre = jnp.dot(tokens, wgu[:, :U], preferred_element_type=F32)
        up_pre = jnp.dot(tokens, wgu[:, U:], preferred_element_type=F32)
        grads_in = xo[1, h, j : j + n].reshape(rows, D)
        hidden = weight * jnp.dot(grads_in, wd[...], preferred_element_type=F32)
        sig = jax.nn.sigmoid(gate_pre)
        up_grad = (hidden * (gate_pre * sig)).astype(BF16)
        gate_grad = (hidden * up_pre * sig * (1.0 + gate_pre * (1.0 - sig))).astype(BF16)
        both = jnp.concatenate([gate_grad, up_grad], axis=1)
        dg[h, j : j + n] = both.reshape(n, 2, HALF, 2 * U)

        def tile(i, carry):
            cols = pl.ds(pl.multiple_of(i * TILE, TILE), TILE)
            part = lax.dot_general(
                dg[h, j : j + n].reshape(rows, 2 * U), wgu[cols, :], (((1,), (1,)), ((), ())),
                preferred_element_type=F32,
            ).astype(BF16).reshape(n, 2, HALF, TILE)
            s[h, j : j + n, :, cols] = part[:, 0]
            ps[h, j : j + n, :, cols] = part[:, 1]
            return carry

        lax.fori_loop(0, D // TILE, tile, 0)

    def swap_parts(h, j, n):
        return send(ps.at[h, pl.ds(j, n)], pr.at[h, pl.ds(j, n)], sib)

    def scatter_x(h, j, n, swapped):
        swapped.wait_recv()
        for jj in range(j, j + n):
            s[h, jj] = (s[h, jj].astype(F32) + pr[h, jj].astype(F32)).astype(BF16)
        got = []
        for d in (1, 3, 2):
            rows = pl.ds(pl.multiple_of(x_at[d] * XROWS, XROWS), XROWS)
            got.append(
                send(s.at[h, pl.ds(j, n), rows], xr.at[d - 1, h, pl.ds(j, n)], to_x[d])
            )
        return got

    y_got = {0: [], 1: []}
    y_dist = {UP: 1, DOWN: 3, FAR: 2}

    def sum_x(h, j, n, got):
        for copy in got:
            copy.wait_recv()
        rows = pl.ds(pl.multiple_of(x * XROWS, XROWS), XROWS)
        for jj in range(j, j + n):
            total = s[h, jj, rows].astype(F32)
            for d in range(3):
                total = total + xr[d, h, jj].astype(F32)
            u[h, jj] = total.astype(BF16)
            if jj != OWN:
                y_got[h].append(send(u.at[h, jj], yr.at[h, jj - 1], to_y[y_dist[jj]]))

    def scatter_z(h):
        for copy in y_got[h]:
            copy.wait_recv()
        total = u[h, OWN].astype(F32)
        for j in range(3):
            total = total + yr[h, j].astype(F32)
        v[h] = total.astype(BF16)
        got = []
        for d in (4, 3, 5, 2, 6, 1, 7):
            cols = pl.ds(pl.multiple_of(z_at[d] * ZCOLS, ZCOLS), ZCOLS)
            got.append(send(v.at[h, :, cols], zr.at[d - 1, h], to_z[d]))
        return got

    def place(h):
        return pl.ds(pl.multiple_of(h * HALF + x * XROWS, XROWS), XROWS)

    def gather_z(h, got):
        for copy in got:
            copy.wait_recv()
        total = v[h, :, z_cols].astype(F32)
        for d in range(NZ - 1):
            total = total + zr[d, h].astype(F32)
        out[place(h), z_cols] = total.astype(BF16)
        piece = out.at[place(h), z_cols]
        return [send(piece, piece, to_z[d]) for d in (4, 3, 5, 2, 6, 1, 7)]

    def gather_x(h, got):
        for copy in got:
            copy.wait_recv()
        piece = out.at[place(h)]
        return [send(piece, piece, to_x[d]) for d in (1, 3, 2)]

    def grad_tiles(first, last):
        def tile(i, carry):
            cols = pl.ds(pl.multiple_of(i * TILE, TILE), TILE)
            part = lax.dot_general(
                xo[0, :, :, :, :, cols].reshape(8 * TOK, TILE),
                dg[...].reshape(8 * TOK, 2 * U),
                (((0,), (0,)), ((), ())),
                preferred_element_type=F32,
            )
            gg[0, cols] = part[:, :U]
            gu[0, cols] = part[:, U:]
            return carry

        lax.fori_loop(first, last, tile, 0)

    g_swap[OWN].wait_recv()
    for copy in weight_loads:
        copy.wait()
    compute(0, OWN, 1)
    p_own0 = swap_parts(0, OWN, 1)
    far_0, near_0 = share(0, small_0)
    small_1 = send_small(1)
    compute(1, OWN, 1)
    p_own1 = swap_parts(1, OWN, 1)
    for j, _ in TO_Y:
        g_move[j].wait_recv()
        g_swap[j] = send(g8.at[j, 0], g8.at[j, 1], sib)
    x_own0 = scatter_x(0, OWN, 1, p_own0)
    x_own1 = scatter_x(1, OWN, 1, p_own1)
    for j, _ in TO_Y:
        g_swap[j].wait_recv()
    direct_arrive(0, direct_0)
    direct_1 = send_direct(1)
    direct_swap(0)
    far_1, near_1 = share(1, small_1)
    shared_arrive(0, near_0)
    compute(0, UP, 2)
    p_near0 = swap_parts(0, UP, 2)
    far_arrive(0, far_0)
    sum_x(0, OWN, 1, x_own0)
    x_near0 = scatter_x(0, UP, 2, p_near0)
    compute(0, FAR, 1)
    p_far0 = swap_parts(0, FAR, 1)
    sum_x(1, OWN, 1, x_own1)
    x_far0 = scatter_x(0, FAR, 1, p_far0)
    far_arrive(1, far_1)
    sum_x(0, UP, 2, x_near0)
    compute(1, FAR, 1)
    p_far1 = swap_parts(1, FAR, 1)
    sum_x(0, FAR, 1, x_far0)
    x_far1 = scatter_x(1, FAR, 1, p_far1)
    direct_arrive(1, direct_1)
    direct_swap(1)
    shared_arrive(1, near_1)
    z_0 = scatter_z(0)
    compute(1, UP, 1)
    p_up1 = swap_parts(1, UP, 1)
    compute(1, DOWN, 1)
    p_down1 = swap_parts(1, DOWN, 1)
    x_up1 = scatter_x(1, UP, 1, p_up1)
    x_down1 = scatter_x(1, DOWN, 1, p_down1)
    zg_0 = gather_z(0, z_0)
    sum_x(1, FAR, 1, x_far1)
    grad_tiles(0, 2)
    xg_0 = gather_x(0, zg_0)
    grad_tiles(2, 4)
    sum_x(1, UP, 1, x_up1)
    sum_x(1, DOWN, 1, x_down1)
    grad_tiles(4, 6)
    z_1 = scatter_z(1)
    grad_tiles(6, 8)
    zg_1 = gather_z(1, z_1)
    grad_tiles(8, 10)
    xg_1 = gather_x(1, zg_1)
    grad_tiles(10, 12)
    for copy in xg_0 + xg_1:
        copy.wait_recv()
    for copy in sent:
        copy.wait_send()


N_SEND = 128


def local(out_grad, routes, gate_values, layer_input, w_gate, w_up, w_down):
    any_spec = pl.BlockSpec(memory_space=pl.ANY)
    vmem = pl.BlockSpec(memory_space=pltpu.VMEM)
    return pl.pallas_call(
        kernel,
        out_shape=(
            pltpu.VMEM((TOK, D), BF16),
            pltpu.VMEM((1, D, U), F32),
            pltpu.VMEM((1, D, U), F32),
        ),
        in_specs=[any_spec, vmem, vmem, any_spec, any_spec, any_spec, any_spec],
        out_specs=(vmem, vmem, vmem),
        scratch_shapes=[
            pltpu.VMEM((2, 2, 4, 2, HALF, D), BF16),
            pltpu.VMEM((D, 2 * U), BF16),
            pltpu.VMEM((D, U), BF16),
            pltpu.VMEM((4, 2, EXPERTS, TOK), F32),
            pltpu.VMEM((2, 4, 2, HALF, 2 * U), BF16),
            pltpu.VMEM((2, 4, HALF, D), BF16),
            pltpu.VMEM((2, 4, HALF, D), BF16),
            pltpu.VMEM((2, 4, HALF, D), BF16),
            pltpu.VMEM((3, 2, 4, XROWS, D), BF16),
            pltpu.VMEM((2, 4, XROWS, D), BF16),
            pltpu.VMEM((NZ - 1, 2, XROWS, ZCOLS), BF16),
            pltpu.VMEM((2, XROWS, D), BF16),
            pltpu.VMEM((2, 3, XROWS, D), BF16),
            pltpu.SemaphoreType.DMA((8,)),
            pltpu.SemaphoreType.DMA((N_SEND,)),
            pltpu.SemaphoreType.DMA((N_SEND,)),
        ],
        compiler_params=pltpu.CompilerParams(
            collective_id=0, has_side_effects=True, vmem_limit_bytes=56 * 2**20
        ),
        cost_estimate=pl.CostEstimate(
            flops=7 * 2 * 1024 * D * U, bytes_accessed=14 * 2**20, transcendentals=1024 * U
        ),
    )(out_grad, routes.T, gate_values.T, layer_input, w_gate, w_up, w_down)


def solution(mesh):
    placed = (
        P("expert", None),
        P("expert", None),
        P("expert", None),
        P("expert", None),
        P("expert", None, "dp"),
        P("expert", None, "dp"),
        P("expert", None, "dp"),
    )
    return jax.shard_map(
        local,
        mesh=mesh,
        in_specs=placed,
        out_specs=(P("expert", None), P("expert", None, "dp"), P("expert", None, "dp")),
        check_vma=False,
    )
```

```python
import functools

import jax
import jax.numpy as jnp
from jax import lax
from jax.experimental import pallas as pl
from jax.experimental.pallas import tpu as pltpu
from jax.sharding import PartitionSpec as P

MESH = pl.DeviceIdType.MESH
BF16, F32 = jnp.bfloat16, jnp.float32
EXPERTS = 8
NX, NY, NZ = 4, 4, 8
TOK, D, U = 128, 3072, 256
HALF = TOK // 2
XCOLS = D // NX
ZROWS = 16
ZCOLS = XCOLS // 2
FAR_COLS = D // NZ
OWN, UP, DOWN, FAR = 0, 1, 2, 3
TO_Y = ((FAR, 2), (DOWN, 1), (UP, 3))
NEAR = ((DOWN, 1), (UP, 3))
TILE, BACK, TURN = 256, 1536, 512
X_ORDER, Z_ORDER = (2, 1, 3), (4, 3, 5, 2, 6, 1, 7)
NEAR_X, FAR_X = 1, 1


def kernel(
    og_in, routes_in, gates_in, x_in, wg_in, wu_in, wd_in,
    out, gg, gu,
    xo, wgu, wgu_t, wd, g8, dg, ps, pr, s, xr, u, zr, v, yr, yf,
    load_sem, send_sem, recv_sem,
):
    dp, ex = lax.axis_index("dp"), lax.axis_index("expert")
    x, z = lax.rem(dp, NX), lax.div(dp, NX)
    y, c = lax.div(ex, 2), lax.rem(ex, 2)

    def dev(nx, ny, nz, nc):
        return (nz * NX + nx, ny * 2 + nc)

    sib = dev(x, y, z, 1 - c)
    y_at = {d: lax.rem(y + d, NY) for d in (1, 2, 3)}
    x_at = {d: lax.rem(x + d, NX) for d in (1, 2, 3)}
    z_at = {d: lax.rem(z + d, NZ) for d in range(1, NZ)}
    to_y = {d: dev(x, y_at[d], z, c) for d in y_at}
    to_x = {d: dev(x_at[d], y, z, c) for d in x_at}
    to_z = {d: dev(x, y, z_at[d], c) for d in z_at}

    loads = []

    def load(src, dst):
        assert len(loads) < 8
        copy = pltpu.make_async_copy(src, dst, load_sem.at[len(loads)])
        copy.start()
        loads.append(copy)
        return copy

    sent = []

    def send(src, dst, device):
        i = len(sent)
        assert i < N_SEND
        copy = pltpu.make_async_remote_copy(
            src_ref=src, dst_ref=dst, send_sem=send_sem.at[i], recv_sem=recv_sem.at[i],
            device_id=device, device_id_type=MESH,
        )
        copy.start()
        sent.append(copy)
        return copy

    own_loads = {}
    for h in range(2):
        for a, ref in ((0, x_in), (1, og_in)):
            own_loads[a, h] = load(ref.at[pl.ds(h * HALF, HALF)], xo.at[a, h, OWN, 0])
    weight_loads = [
        load(wg_in.at[0], wgu.at[:, pl.ds(0, U)]),
        load(wu_in.at[0], wgu.at[:, pl.ds(U, U)]),
        load(wd_in.at[0], wd),
    ]

    peers = [sib] + list(to_y.values()) + list(to_x.values()) + list(to_z.values())
    barrier = pltpu.get_barrier_semaphore()
    for device in peers:
        pl.semaphore_signal(barrier, inc=1, device_id=device, device_id_type=MESH)

    lane = lax.broadcasted_iota(jnp.int32, (TOK, TOK), 1)
    row = lax.broadcasted_iota(jnp.int32, (TOK, TOK), 0)
    for e in range(EXPERTS):
        g8[OWN, 0, e : e + 1, :] = jnp.sum(
            jnp.where(routes_in[...] == e, gates_in[...], 0.0), axis=0, keepdims=True
        )

    pl.semaphore_wait(barrier, len(peers))

    g_move = {j: send(g8.at[OWN, 0], g8.at[j, 0], to_y[d]) for j, d in TO_Y}
    g_swap = {OWN: send(g8.at[OWN, 0], g8.at[OWN, 1], sib)}
    x_cols = pl.ds(pl.multiple_of(x * XCOLS, XCOLS), XCOLS)
    z_cols = pl.ds(pl.multiple_of(z * FAR_COLS, FAR_COLS), FAR_COLS)

    def groups(first, count):
        return pl.ds(first * 16, count * 16)

    near_x = groups(4 - NEAR_X, NEAR_X)
    far_x, far_z = groups(0, FAR_X), groups(FAR_X, 4 - FAR_X)

    def move(h, j, rows, cols, device):
        piece = xo.at[:, h, OWN, 0, rows, cols]
        return send(piece, xo.at[:, h, j, 0, rows, cols], device)

    swap, swapped = {}, set()

    def do_swap(h, j, first, count):
        rows = groups(first, count)
        copy = send(xo.at[:, h, j, 0, rows], xo.at[:, h, j, 1, rows], sib)
        for g in range(first, first + count):
            swap[h, j, g] = copy

    def swap_wait(h, j, first, count):
        for g in range(first, first + count):
            if id(swap[h, j, g]) not in swapped:
                swapped.add(id(swap[h, j, g]))
                swap[h, j, g].wait_recv()

    def wait_all(copies):
        for copy in copies:
            copy.wait_recv()

    def send_small(h):
        far = []
        if FAR_X < 4:
            far.append(move(h, FAR, far_z, z_cols, to_y[2]))
        if FAR_X:
            far.append(move(h, FAR, far_x, x_cols, to_y[2]))
        near = [move(h, j, near_x, x_cols, to_y[d]) for j, d in NEAR if NEAR_X]
        return far, near

    def send_direct(h, first, count):
        return [move(h, j, groups(first, count), slice(None), to_y[d]) for j, d in NEAR]

    def share(h, small):
        far, near = small
        wait_all(far)
        far_got, near_got = [], []
        for d in Z_ORDER if FAR_X < 4 else ():
            piece = xo.at[:, h, FAR, 0, far_z, z_cols]
            far_got.append(send(piece, piece, to_z[d]))
        for d in X_ORDER:
            if FAR_X:
                piece = xo.at[:, h, FAR, 0, far_x, x_cols]
                far_got.append(send(piece, piece, to_x[d]))
        wait_all(near)
        for d in X_ORDER:
            if NEAR_X:
                piece = xo.at[:, h, pl.ds(UP, 2), 0, near_x, x_cols]
                near_got.append(send(piece, piece, to_x[d]))
        return far_got, near_got

    def far_arrive(h, got):
        wait_all(got)
        do_swap(h, FAR, 0, 4)

    def near_arrive(h, got, first, count):
        wait_all(got)
        for j, _ in NEAR:
            do_swap(h, j, first, count)

    for a in range(2):
        own_loads[a, 0].wait()
    small_0 = send_small(0)
    for a in range(2):
        own_loads[a, 1].wait()
    small_1 = send_small(1)
    first_0 = send_direct(0, 0, 2)
    second_0 = send_direct(0, 2, 2 - NEAR_X)
    do_swap(0, OWN, 0, 4)
    do_swap(1, OWN, 0, 4)

    def weight_column(h, j, slot, first, count):
        mine = lax.broadcasted_iota(jnp.int32, (EXPERTS, TOK), 0) == ex
        line = jnp.sum(jnp.where(mine, g8[j, slot], 0.0), axis=0, keepdims=True)
        whole = jnp.sum(jnp.where(lane == row, line, 0.0), axis=1, keepdims=True)
        start = h * HALF + first * 16
        return whole[start : start + count * 16]

    def compute(h, j, n, first, count):
        rows, sub = n * 2 * count * 16, groups(first, count)
        for jj in range(j, j + n):
            swap_wait(h, jj, first, count)
        weight = jnp.concatenate(
            [weight_column(h, jj, slot, first, count) for jj in range(j, j + n) for slot in range(2)],
            axis=0,
        )
        tokens = xo[0, h, j : j + n, :, sub].reshape(rows, D)
        gate_pre = jnp.dot(tokens, wgu[:, :U], preferred_element_type=F32)
        up_pre = jnp.dot(tokens, wgu[:, U:], preferred_element_type=F32)
        grads_in = xo[1, h, j : j + n, :, sub].reshape(rows, D)
        hidden = weight * jnp.dot(grads_in, wd[...], preferred_element_type=F32)
        sig = jax.nn.sigmoid(gate_pre)
        up_grad = (hidden * (gate_pre * sig)).astype(BF16)
        gate_grad = (hidden * up_pre * sig * (1.0 + gate_pre * (1.0 - sig))).astype(BF16)
        both = jnp.concatenate([gate_grad, up_grad], axis=1)
        dg[h, j : j + n, :, sub] = both.reshape(n, 2, count * 16, 2 * U)

        def tile(i, carry):
            cols = pl.ds(pl.multiple_of(i * BACK, BACK), BACK)
            part = jnp.dot(both, wgu_t[:, cols], preferred_element_type=F32)
            part = part.astype(BF16).reshape(n, 2, count * 16, BACK)
            s[h, j : j + n, sub, cols] = part[:, 0]
            ps[h, j : j + n, sub, cols] = part[:, 1]
            return carry

        lax.fori_loop(0, D // BACK, tile, 0)
        piece = (h, pl.ds(j, n), sub)
        return send(ps.at[piece], pr.at[piece], sib)

    def merge(h, j, n, first, count, parts):
        sub = groups(first, count)
        parts.wait_recv()
        for jj in range(j, j + n):
            s[h, jj, sub] = (s[h, jj, sub].astype(F32) + pr[h, jj, sub].astype(F32)).astype(BF16)

    def send_x(h, j, n, first, count):
        sub = groups(first, count)
        got = []
        for d in X_ORDER:
            cols = pl.ds(pl.multiple_of(x_at[d] * XCOLS, XCOLS), XCOLS)
            got.append(
                send(s.at[h, pl.ds(j, n), sub, cols], xr.at[d - 1, h, pl.ds(j, n), sub], to_x[d])
            )
        return got

    def scatter_x(h, j, n, first, count, parts):
        merge(h, j, n, first, count, parts)
        return send_x(h, j, n, first, count)

    def scatter_near(h, j, n, first, count, parts):
        merge(h, j, n, first, count, parts)
        sub = groups(first, count)
        return [
            send(s.at[h, UP, sub], yf.at[0, sub], to_y[1]),
            send(s.at[h, DOWN, sub], yf.at[1, sub], to_y[3]),
        ]

    def sum_near(h, j, n, first, count, got):
        wait_all(got)
        sub = groups(first, count)
        total = s[h, OWN, sub].astype(F32) + yf[0, sub].astype(F32) + yf[1, sub].astype(F32)
        s[h, OWN, sub] = total.astype(BF16)
        return send_x(h, OWN, 1, first, count)

    y_got = {0: [], 1: []}
    y_dist = {UP: 1, DOWN: 3, FAR: 2}

    def sum_x(h, j, n, first, count, got):
        sub = groups(first, count)
        wait_all(got)
        for jj in range(j, j + n):
            total = s[h, jj, sub, x_cols].astype(F32)
            for d in range(3):
                total = total + xr[d, h, jj, sub].astype(F32)
            u[h, jj, sub] = total.astype(BF16)
            if jj != OWN:
                y_got[h].append(send(u.at[h, jj, sub], yr.at[h, jj - 1, sub], to_y[y_dist[jj]]))

    def z_part(nz):
        rows = pl.ds(pl.multiple_of(lax.rem(nz, 4) * ZROWS, ZROWS), ZROWS)
        return rows, pl.ds(pl.multiple_of(lax.div(nz, 4) * ZCOLS, ZCOLS), ZCOLS)

    def scatter_z(h):
        wait_all(y_got[h])
        total = u[h, OWN].astype(F32)
        for j in range(3) if h == 0 else (FAR - 1,):
            total = total + yr[h, j].astype(F32)
        v[h] = total.astype(BF16)
        got = []
        for d in Z_ORDER:
            rows, cols = z_part(z_at[d])
            got.append(send(v.at[h, rows, cols], zr.at[d - 1, h], to_z[d]))
        return got

    def gather_z(h, got):
        wait_all(got)
        rows, cols = z_part(z)
        total = v[h, rows, cols].astype(F32)
        for d in range(NZ - 1):
            total = total + zr[d, h].astype(F32)
        rows = pl.ds(pl.multiple_of(h * HALF + lax.rem(z, 4) * ZROWS, ZROWS), ZROWS)
        cols = pl.ds(pl.multiple_of(x * XCOLS + lax.div(z, 4) * ZCOLS, ZCOLS), ZCOLS)
        out[rows, cols] = total.astype(BF16)
        piece = out.at[rows, cols]
        return [send(piece, piece, to_z[d]) for d in Z_ORDER]

    def gather_x(h, got):
        wait_all(got)
        piece = out.at[pl.ds(h * HALF, HALF), x_cols]
        return [send(piece, piece, to_x[d]) for d in X_ORDER]

    def grad_tiles(first, last):
        def tile(i, carry):
            cols = pl.ds(pl.multiple_of(i * TILE, TILE), TILE)
            part = lax.dot_general(
                xo[0, :, :, :, :, cols].reshape(8 * TOK, TILE),
                dg[...].reshape(8 * TOK, 2 * U),
                (((0,), (0,)), ((), ())),
                preferred_element_type=F32,
            )
            gg[0, cols] = part[:, :U]
            gu[0, cols] = part[:, U:]
            return carry

        lax.fori_loop(first, last, tile, 0)

    own0, own1 = (0, OWN, 1, 0, 4), (1, OWN, 1, 0, 4)
    near0, far0, far1 = (0, UP, 2, 0, 4), (0, FAR, 1, 0, 4), (1, FAR, 1, 0, 4)
    first1, second1 = (1, UP, 2, 0, 2), (1, UP, 2, 2, 2)

    for copy in weight_loads:
        copy.wait()

    def turn(i, carry):
        cols = pl.ds(pl.multiple_of(i * TURN, TURN), TURN)
        wgu_t[:, cols] = wgu[cols, :].T
        return carry

    lax.fori_loop(0, D // TURN, turn, 0)
    g_swap[OWN].wait_recv()
    p_own0 = compute(*own0)
    far_0, shared_0 = share(0, small_0)
    far_1, shared_1 = share(1, small_1)
    p_own1 = compute(*own1)
    for j, _ in TO_Y:
        g_move[j].wait_recv()
        g_swap[j] = send(g8.at[j, 0], g8.at[j, 1], sib)
    x_own0 = scatter_x(*own0, p_own0)
    merge(*own1, p_own1)
    near_arrive(0, first_0, 0, 2)
    first_1 = send_direct(1, 0, 2)
    near_arrive(0, second_0, 2, 2 - NEAR_X)
    second_1 = send_direct(1, 2, 2 - NEAR_X)
    if NEAR_X:
        near_arrive(0, shared_0, 4 - NEAR_X, NEAR_X)
    for j, _ in TO_Y:
        g_swap[j].wait_recv()
    p_near0 = compute(*near0)
    sum_x(*own0, x_own0)
    x_near0 = scatter_x(*near0, p_near0)
    far_arrive(0, far_0)
    p_far0 = compute(*far0)
    near_arrive(1, first_1, 0, 2)
    x_far0 = scatter_x(*far0, p_far0)
    p_first1 = compute(*first1)
    far_arrive(1, far_1)
    y_first1 = scatter_near(*first1, p_first1)
    sum_x(*near0, x_near0)
    p_far1 = compute(*far1)
    near_arrive(1, second_1, 2, 2 - NEAR_X)
    if NEAR_X:
        near_arrive(1, shared_1, 4 - NEAR_X, NEAR_X)
    x_far1 = scatter_x(*far1, p_far1)
    p_second1 = compute(*second1)
    sum_x(*far0, x_far0)
    x_first1 = sum_near(*first1, y_first1)
    y_second1 = scatter_near(*second1, p_second1)
    z_0 = scatter_z(0)
    grad_tiles(0, 2)
    sum_x(*far1, x_far1)
    zg_0 = gather_z(0, z_0)
    grad_tiles(2, 4)
    x_second1 = sum_near(*second1, y_second1)
    sum_x(1, OWN, 1, 0, 2, x_first1)
    grad_tiles(4, 6)
    sum_x(1, OWN, 1, 2, 2, x_second1)
    xg_0 = gather_x(0, zg_0)
    z_1 = scatter_z(1)
    grad_tiles(6, 9)
    zg_1 = gather_z(1, z_1)
    grad_tiles(9, 12)
    xg_1 = gather_x(1, zg_1)
    wait_all(xg_0 + xg_1)
    for copy in sent:
        copy.wait_send()


N_SEND = 144


def local(out_grad, routes, gate_values, layer_input, w_gate, w_up, w_down):
    any_spec = pl.BlockSpec(memory_space=pl.ANY)
    vmem = pl.BlockSpec(memory_space=pltpu.VMEM)
    return pl.pallas_call(
        kernel,
        out_shape=(
            pltpu.VMEM((TOK, D), BF16),
            pltpu.VMEM((1, D, U), F32),
            pltpu.VMEM((1, D, U), F32),
        ),
        in_specs=[any_spec, vmem, vmem, any_spec, any_spec, any_spec, any_spec],
        out_specs=(vmem, vmem, vmem),
        scratch_shapes=[
            pltpu.VMEM((2, 2, 4, 2, HALF, D), BF16),
            pltpu.VMEM((D, 2 * U), BF16),
            pltpu.VMEM((2 * U, D), BF16),
            pltpu.VMEM((D, U), BF16),
            pltpu.VMEM((4, 2, EXPERTS, TOK), F32),
            pltpu.VMEM((2, 4, 2, HALF, 2 * U), BF16),
            pltpu.VMEM((2, 4, HALF, D), BF16),
            pltpu.VMEM((2, 4, HALF, D), BF16),
            pltpu.VMEM((2, 4, HALF, D), BF16),
            pltpu.VMEM((3, 2, 4, HALF, XCOLS), BF16),
            pltpu.VMEM((2, 4, HALF, XCOLS), BF16),
            pltpu.VMEM((NZ - 1, 2, ZROWS, ZCOLS), BF16),
            pltpu.VMEM((2, HALF, XCOLS), BF16),
            pltpu.VMEM((2, 3, HALF, XCOLS), BF16),
            pltpu.VMEM((2, HALF, D), BF16),
            pltpu.SemaphoreType.DMA((8,)),
            pltpu.SemaphoreType.DMA((N_SEND,)),
            pltpu.SemaphoreType.DMA((N_SEND,)),
        ],
        compiler_params=pltpu.CompilerParams(
            collective_id=0, has_side_effects=True, vmem_limit_bytes=56 * 2**20
        ),
        cost_estimate=pl.CostEstimate(
            flops=7 * 2 * 1024 * D * U, bytes_accessed=14 * 2**20, transcendentals=1024 * U
        ),
    )(out_grad, routes.T, gate_values.T, layer_input, w_gate, w_up, w_down)


def solution(mesh):
    placed = (
        P("expert", None),
        P("expert", None),
        P("expert", None),
        P("expert", None),
        P("expert", None, "dp"),
        P("expert", None, "dp"),
        P("expert", None, "dp"),
    )
    return jax.shard_map(
        local,
        mesh=mesh,
        in_specs=placed,
        out_specs=(P("expert", None), P("expert", None, "dp"), P("expert", None, "dp")),
        check_vma=False,
    )
```

```python
import functools

import jax
import jax.numpy as jnp
from jax import lax
from jax.experimental import pallas as pl
from jax.experimental.pallas import tpu as pltpu
from jax.sharding import PartitionSpec as P

MESH = pl.DeviceIdType.MESH
BF16, F32 = jnp.bfloat16, jnp.float32
EXPERTS = 8
NX, NY, NZ = 4, 4, 8
TOK, D, U = 128, 3072, 256
HALF = TOK // 2
XCOLS = D // NX
ZROWS = 16
ZCOLS = XCOLS // 2
FAR_COLS = D // NZ
OWN, UP, DOWN, FAR = 0, 1, 2, 3
TO_Y = ((FAR, 2), (DOWN, 1), (UP, 3))
NEAR = ((DOWN, 1), (UP, 3))
TILE, BACK, TURN = 256, 1536, 512
X_ORDER, Z_ORDER = (2, 1, 3), (4, 3, 5, 2, 6, 1, 7)
NEAR_X, FAR_X = 1, 1


def kernel(
    og_in, routes_in, gates_in, x_in, wg_in, wu_in, wd_in,
    out, gg, gu,
    xo, wgu, wgu_t, wd, g8, dg, ps, pr, s, xr, u, zr, v, yr, yf,
    load_sem, send_sem, recv_sem,
):
    dp, ex = lax.axis_index("dp"), lax.axis_index("expert")
    x, z = lax.rem(dp, NX), lax.div(dp, NX)
    y, c = lax.div(ex, 2), lax.rem(ex, 2)

    def dev(nx, ny, nz, nc):
        return (nz * NX + nx, ny * 2 + nc)

    sib = dev(x, y, z, 1 - c)
    y_at = {d: lax.rem(y + d, NY) for d in (1, 2, 3)}
    x_at = {d: lax.rem(x + d, NX) for d in (1, 2, 3)}
    z_at = {d: lax.rem(z + d, NZ) for d in range(1, NZ)}
    to_y = {d: dev(x, y_at[d], z, c) for d in y_at}
    to_x = {d: dev(x_at[d], y, z, c) for d in x_at}
    to_z = {d: dev(x, y, z_at[d], c) for d in z_at}

    peers = [sib] + list(to_y.values()) + list(to_x.values()) + list(to_z.values())
    barrier = pltpu.get_barrier_semaphore()
    for device in peers:
        pl.semaphore_signal(barrier, inc=1, device_id=device, device_id_type=MESH)

    loads = []

    def load(src, dst):
        assert len(loads) < 8
        copy = pltpu.make_async_copy(src, dst, load_sem.at[len(loads)])
        copy.start()
        loads.append(copy)
        return copy

    sent = []

    def make(src, dst, device, condition=None):
        i = len(sent)
        assert i < N_SEND
        copy = pltpu.make_async_remote_copy(
            src_ref=src, dst_ref=dst, send_sem=send_sem.at[i], recv_sem=recv_sem.at[i],
            device_id=device, device_id_type=MESH,
        )
        sent.append((copy, condition))
        return copy

    def send(src, dst, device):
        copy = make(src, dst, device)
        copy.start()
        return copy

    own_loads = {}
    for h in range(2):
        for a, ref in ((0, x_in), (1, og_in)):
            own_loads[a, h] = load(ref.at[pl.ds(h * HALF, HALF)], xo.at[a, h, OWN, 0])
    weight_loads = [
        load(wg_in.at[0], wgu.at[:, pl.ds(0, U)]),
        load(wu_in.at[0], wgu.at[:, pl.ds(U, U)]),
        load(wd_in.at[0], wd),
    ]

    lane = lax.broadcasted_iota(jnp.int32, (TOK, TOK), 1)
    row = lax.broadcasted_iota(jnp.int32, (TOK, TOK), 0)
    for e in range(EXPERTS):
        g8[OWN, 0, e : e + 1, :] = jnp.sum(
            jnp.where(routes_in[...] == e, gates_in[...], 0.0), axis=0, keepdims=True
        )

    pl.semaphore_wait(barrier, len(peers))
    g_move = {j: send(g8.at[OWN, 0], g8.at[j, 0], to_y[d]) for j, d in TO_Y}
    g_swap = {OWN: send(g8.at[OWN, 0], g8.at[OWN, 1], sib)}

    x_cols = pl.ds(pl.multiple_of(x * XCOLS, XCOLS), XCOLS)
    z_cols = pl.ds(pl.multiple_of(z * FAR_COLS, FAR_COLS), FAR_COLS)

    def groups(first, count):
        return pl.ds(first * 16, count * 16)

    near_x = groups(4 - NEAR_X, NEAR_X)
    far_x, far_z = groups(0, FAR_X), groups(FAR_X, 4 - FAR_X)

    def move(h, j, rows, cols, device):
        piece = xo.at[:, h, OWN, 0, rows, cols]
        return send(piece, xo.at[:, h, j, 0, rows, cols], device)

    swap, swapped = {}, set()

    def do_swap(h, j, first, count):
        rows = groups(first, count)
        copy = send(xo.at[:, h, j, 0, rows], xo.at[:, h, j, 1, rows], sib)
        for g in range(first, first + count):
            swap[h, j, g] = copy

    def swap_wait(h, j, first, count):
        for g in range(first, first + count):
            if id(swap[h, j, g]) not in swapped:
                swapped.add(id(swap[h, j, g]))
                swap[h, j, g].wait_recv()

    def wait_all(copies):
        for copy in copies:
            copy.wait_recv()

    def send_small(h):
        far = []
        if FAR_X < 4:
            far.append(move(h, FAR, far_z, z_cols, to_y[2]))
        if FAR_X:
            far.append(move(h, FAR, far_x, x_cols, to_y[2]))
        near = [move(h, j, near_x, x_cols, to_y[d]) for j, d in NEAR if NEAR_X]
        return far, near

    def send_direct(h, first, count):
        return [move(h, j, groups(first, count), slice(None), to_y[d]) for j, d in NEAR]

    def share(h, small):
        far, near = small
        wait_all(far)
        far_got, near_got = [], []
        for d in Z_ORDER if FAR_X < 4 else ():
            piece = xo.at[:, h, FAR, 0, far_z, z_cols]
            far_got.append(send(piece, piece, to_z[d]))
        for d in X_ORDER:
            if FAR_X:
                piece = xo.at[:, h, FAR, 0, far_x, x_cols]
                far_got.append(send(piece, piece, to_x[d]))
        wait_all(near)
        for d in X_ORDER:
            if NEAR_X:
                piece = xo.at[:, h, pl.ds(UP, 2), 0, near_x, x_cols]
                near_got.append(send(piece, piece, to_x[d]))
        return far_got, near_got

    def far_arrive(h, got):
        wait_all(got)
        do_swap(h, FAR, 0, 4)

    def near_arrive(h, got, first, count):
        wait_all(got)
        for j, _ in NEAR:
            do_swap(h, j, first, count)

    for a in range(2):
        own_loads[a, 0].wait()
    small_0 = send_small(0)
    for a in range(2):
        own_loads[a, 1].wait()
    small_1 = send_small(1)
    first_0 = send_direct(0, 0, 2)
    second_0 = send_direct(0, 2, 2 - NEAR_X)
    do_swap(0, OWN, 0, 4)
    do_swap(1, OWN, 0, 4)

    def weight_column(h, j, slot, first, count):
        mine = lax.broadcasted_iota(jnp.int32, (EXPERTS, TOK), 0) == ex
        line = jnp.sum(jnp.where(mine, g8[j, slot], 0.0), axis=0, keepdims=True)
        whole = jnp.sum(jnp.where(lane == row, line, 0.0), axis=1, keepdims=True)
        start = h * HALF + first * 16
        return whole[start : start + count * 16]

    def compute(h, j, n, first, count):
        rows, sub = n * 2 * count * 16, groups(first, count)
        for jj in range(j, j + n):
            swap_wait(h, jj, first, count)
        weight = jnp.concatenate(
            [weight_column(h, jj, slot, first, count) for jj in range(j, j + n) for slot in range(2)],
            axis=0,
        )
        tokens = xo[0, h, j : j + n, :, sub].reshape(rows, D)
        gate_pre = jnp.dot(tokens, wgu[:, :U], preferred_element_type=F32)
        up_pre = jnp.dot(tokens, wgu[:, U:], preferred_element_type=F32)
        grads_in = xo[1, h, j : j + n, :, sub].reshape(rows, D)
        hidden = weight * jnp.dot(grads_in, wd[...], preferred_element_type=F32)
        sig = jax.nn.sigmoid(gate_pre)
        up_grad = (hidden * (gate_pre * sig)).astype(BF16)
        gate_grad = (hidden * up_pre * sig * (1.0 + gate_pre * (1.0 - sig))).astype(BF16)
        both = jnp.concatenate([gate_grad, up_grad], axis=1)
        dg[h, j : j + n, :, sub] = both.reshape(n, 2, count * 16, 2 * U)

        def tile(i, carry):
            cols = pl.ds(pl.multiple_of(i * BACK, BACK), BACK)
            part = jnp.dot(both, wgu_t[:, cols], preferred_element_type=F32)
            part = part.astype(BF16).reshape(n, 2, count * 16, BACK)
            s[h, j : j + n, sub, cols] = part[:, 0]
            ps[h, j : j + n, sub, cols] = part[:, 1]
            return carry

        lax.fori_loop(0, D // BACK, tile, 0)
        piece = (h, pl.ds(j, n), sub)
        return send(ps.at[piece], pr.at[piece], sib)

    def merge(h, j, n, first, count, parts):
        sub = groups(first, count)
        parts.wait_recv()
        for jj in range(j, j + n):
            s[h, jj, sub] = (s[h, jj, sub].astype(F32) + pr[h, jj, sub].astype(F32)).astype(BF16)

    def send_x(h, j, n, first, count):
        sub = groups(first, count)
        got = []
        for d in X_ORDER:
            cols = pl.ds(pl.multiple_of(x_at[d] * XCOLS, XCOLS), XCOLS)
            got.append(
                send(s.at[h, pl.ds(j, n), sub, cols], xr.at[d - 1, h, pl.ds(j, n), sub], to_x[d])
            )
        return got

    def scatter_x(h, j, n, first, count, parts):
        merge(h, j, n, first, count, parts)
        return send_x(h, j, n, first, count)

    def scatter_near(h, j, n, first, count, parts):
        merge(h, j, n, first, count, parts)
        sub = groups(first, count)
        return [
            send(s.at[h, UP, sub], yf.at[0, sub], to_y[1]),
            send(s.at[h, DOWN, sub], yf.at[1, sub], to_y[3]),
        ]

    def sum_near(h, j, n, first, count, got):
        wait_all(got)
        sub = groups(first, count)
        total = s[h, OWN, sub].astype(F32) + yf[0, sub].astype(F32) + yf[1, sub].astype(F32)
        s[h, OWN, sub] = total.astype(BF16)
        return send_x(h, OWN, 1, first, count)

    y_got = {0: [], 1: []}
    y_dist = {UP: 1, DOWN: 3, FAR: 2}

    def sum_x(h, j, n, first, count, got):
        sub = groups(first, count)
        wait_all(got)
        for jj in range(j, j + n):
            total = s[h, jj, sub, x_cols].astype(F32)
            for d in range(3):
                total = total + xr[d, h, jj, sub].astype(F32)
            u[h, jj, sub] = total.astype(BF16)
            if jj != OWN:
                y_got[h].append(send(u.at[h, jj, sub], yr.at[h, jj - 1, sub], to_y[y_dist[jj]]))

    def z_part(nz):
        rows = pl.ds(pl.multiple_of(lax.rem(nz, 4) * ZROWS, ZROWS), ZROWS)
        return rows, pl.ds(pl.multiple_of(lax.div(nz, 4) * ZCOLS, ZCOLS), ZCOLS)

    def scatter_z(h):
        wait_all(y_got[h])
        total = u[h, OWN].astype(F32)
        for j in range(3):
            total = total + yr[h, j].astype(F32)
        v[h] = total.astype(BF16)
        got = []
        for d in Z_ORDER:
            rows, cols = z_part(z_at[d])
            got.append(send(v.at[h, rows, cols], zr.at[d - 1, h], to_z[d]))
        return got

    def gather_z(h, got):
        wait_all(got)
        rows, cols = z_part(z)
        total = v[h, rows, cols].astype(F32)
        for d in range(NZ - 1):
            total = total + zr[d, h].astype(F32)
        rows = pl.ds(pl.multiple_of(h * HALF + lax.rem(z, 4) * ZROWS, ZROWS), ZROWS)
        cols = pl.ds(pl.multiple_of(x * XCOLS + lax.div(z, 4) * ZCOLS, ZCOLS), ZCOLS)
        out[rows, cols] = total.astype(BF16)
        piece = out.at[rows, cols]
        return [send(piece, piece, to_z[d]) for d in Z_ORDER]

    def owns(nz, part):
        return lax.div(lax.rem(nz, 4), 2) == part

    def scatter_z_part(part):
        if part == 0:
            wait_all(y_got[1])
        sub = groups(2 * part, 2)
        v[1, sub] = (u[1, OWN, sub].astype(F32) + yr[1, FAR - 1, sub].astype(F32)).astype(BF16)
        got = []
        for d in Z_ORDER:
            rows, cols = z_part(z_at[d])
            theirs = owns(z_at[d], part)
            copy = make(v.at[1, rows, cols], zr.at[d - 1, 1], to_z[d], theirs)
            pl.when(theirs)(copy.start)
            got.append(copy)
        return got

    def gather_z_part(part, got):
        rows, cols = z_part(z)
        out_rows = pl.ds(pl.multiple_of(HALF + lax.rem(z, 4) * ZROWS, ZROWS), ZROWS)
        out_cols = pl.ds(pl.multiple_of(x * XCOLS + lax.div(z, 4) * ZCOLS, ZCOLS), ZCOLS)
        piece = out.at[out_rows, out_cols]
        mine = owns(z, part)
        gathered = [(d, make(piece, piece, to_z[d], mine)) for d in Z_ORDER]

        @pl.when(mine)
        def _():
            wait_all(got)
            total = v[1, rows, cols].astype(F32)
            for d in range(NZ - 1):
                total = total + zr[d, 1].astype(F32)
            out[out_rows, out_cols] = total.astype(BF16)
            for _, copy in gathered:
                copy.start()

        return gathered

    def gather_x_part(part, gathered):
        for d, copy in gathered:
            pl.when(owns(lax.rem(z + NZ - d, NZ), part))(copy.wait_recv)
        piece = out.at[pl.ds(HALF + part * 2 * ZROWS, 2 * ZROWS), x_cols]
        return [send(piece, piece, to_x[d]) for d in X_ORDER]

    def gather_x(h, got):
        wait_all(got)
        piece = out.at[pl.ds(h * HALF, HALF), x_cols]
        return [send(piece, piece, to_x[d]) for d in X_ORDER]

    def grad_tiles(first, last):
        def tile(i, carry):
            cols = pl.ds(pl.multiple_of(i * TILE, TILE), TILE)
            part = lax.dot_general(
                xo[0, :, :, :, :, cols].reshape(8 * TOK, TILE),
                dg[...].reshape(8 * TOK, 2 * U),
                (((0,), (0,)), ((), ())),
                preferred_element_type=F32,
            )
            gg[0, cols] = part[:, :U]
            gu[0, cols] = part[:, U:]
            return carry

        lax.fori_loop(first, last, tile, 0)

    own0, own1 = (0, OWN, 1, 0, 4), (1, OWN, 1, 0, 4)
    near0, far0, far1 = (0, UP, 2, 0, 4), (0, FAR, 1, 0, 4), (1, FAR, 1, 0, 4)
    first1, second1 = (1, UP, 2, 0, 2), (1, UP, 2, 2, 2)

    for copy in weight_loads:
        copy.wait()

    def turn(i, carry):
        cols = pl.ds(pl.multiple_of(i * TURN, TURN), TURN)
        wgu_t[:, cols] = wgu[cols, :].T
        return carry

    lax.fori_loop(0, D // TURN, turn, 0)
    g_swap[OWN].wait_recv()
    p_own0 = compute(*own0)
    far_0, shared_0 = share(0, small_0)
    far_1, shared_1 = share(1, small_1)
    first_1 = send_direct(1, 0, 2)
    p_own1 = compute(*own1)
    for j, _ in TO_Y:
        g_move[j].wait_recv()
        g_swap[j] = send(g8.at[j, 0], g8.at[j, 1], sib)
    x_own0 = scatter_x(*own0, p_own0)
    merge(*own1, p_own1)
    near_arrive(0, first_0, 0, 2)
    near_arrive(0, second_0, 2, 2 - NEAR_X)
    second_1 = send_direct(1, 2, 2 - NEAR_X)
    if NEAR_X:
        near_arrive(0, shared_0, 4 - NEAR_X, NEAR_X)
    for j, _ in TO_Y:
        g_swap[j].wait_recv()
    p_near0 = compute(*near0)
    sum_x(*own0, x_own0)
    x_near0 = scatter_x(*near0, p_near0)
    far_arrive(0, far_0)
    p_far0 = compute(*far0)
    near_arrive(1, first_1, 0, 2)
    x_far0 = scatter_x(*far0, p_far0)
    p_first1 = compute(*first1)
    far_arrive(1, far_1)
    y_first1 = scatter_near(*first1, p_first1)
    sum_x(*near0, x_near0)
    p_far1 = compute(*far1)
    near_arrive(1, second_1, 2, 2 - NEAR_X)
    if NEAR_X:
        near_arrive(1, shared_1, 4 - NEAR_X, NEAR_X)
    x_far1 = scatter_x(*far1, p_far1)
    p_second1 = compute(*second1)
    sum_x(*far0, x_far0)
    x_first1 = sum_near(*first1, y_first1)
    y_second1 = scatter_near(*second1, p_second1)
    grad_tiles(0, 4)
    z_0 = scatter_z(0)
    sum_x(*far1, x_far1)
    zg_0 = gather_z(0, z_0)
    sum_x(1, OWN, 1, 0, 2, x_first1)
    x_second1 = sum_near(*second1, y_second1)
    z_first = scatter_z_part(0)
    grad_tiles(4, 8)
    zg_first = gather_z_part(0, z_first)
    sum_x(1, OWN, 1, 2, 2, x_second1)
    z_second = scatter_z_part(1)
    xg_0 = gather_x(0, zg_0)
    grad_tiles(8, 10)
    xg_first = gather_x_part(0, zg_first)
    zg_second = gather_z_part(1, z_second)
    grad_tiles(10, 12)
    xg_second = gather_x_part(1, zg_second)
    wait_all(xg_0 + xg_first + xg_second)
    for copy, condition in sent:
        if condition is None:
            copy.wait_send()
        else:
            pl.when(condition)(copy.wait_send)


N_SEND = 160


def local(out_grad, routes, gate_values, layer_input, w_gate, w_up, w_down):
    any_spec = pl.BlockSpec(memory_space=pl.ANY)
    vmem = pl.BlockSpec(memory_space=pltpu.VMEM)
    return pl.pallas_call(
        kernel,
        out_shape=(
            pltpu.VMEM((TOK, D), BF16),
            pltpu.VMEM((1, D, U), F32),
            pltpu.VMEM((1, D, U), F32),
        ),
        in_specs=[any_spec, vmem, vmem, any_spec, any_spec, any_spec, any_spec],
        out_specs=(vmem, vmem, vmem),
        scratch_shapes=[
            pltpu.VMEM((2, 2, 4, 2, HALF, D), BF16),
            pltpu.VMEM((D, 2 * U), BF16),
            pltpu.VMEM((2 * U, D), BF16),
            pltpu.VMEM((D, U), BF16),
            pltpu.VMEM((4, 2, EXPERTS, TOK), F32),
            pltpu.VMEM((2, 4, 2, HALF, 2 * U), BF16),
            pltpu.VMEM((2, 4, HALF, D), BF16),
            pltpu.VMEM((2, 4, HALF, D), BF16),
            pltpu.VMEM((2, 4, HALF, D), BF16),
            pltpu.VMEM((3, 2, 4, HALF, XCOLS), BF16),
            pltpu.VMEM((2, 4, HALF, XCOLS), BF16),
            pltpu.VMEM((NZ - 1, 2, ZROWS, ZCOLS), BF16),
            pltpu.VMEM((2, HALF, XCOLS), BF16),
            pltpu.VMEM((2, 3, HALF, XCOLS), BF16),
            pltpu.VMEM((2, HALF, D), BF16),
            pltpu.SemaphoreType.DMA((8,)),
            pltpu.SemaphoreType.DMA((N_SEND,)),
            pltpu.SemaphoreType.DMA((N_SEND,)),
        ],
        compiler_params=pltpu.CompilerParams(
            collective_id=0, has_side_effects=True, vmem_limit_bytes=56 * 2**20
        ),
        cost_estimate=pl.CostEstimate(
            flops=7 * 2 * 1024 * D * U, bytes_accessed=14 * 2**20, transcendentals=1024 * U
        ),
    )(out_grad, routes.T, gate_values.T, layer_input, w_gate, w_up, w_down)


def solution(mesh):
    placed = (
        P("expert", None),
        P("expert", None),
        P("expert", None),
        P("expert", None),
        P("expert", None, "dp"),
        P("expert", None, "dp"),
        P("expert", None, "dp"),
    )
    return jax.shard_map(
        local,
        mesh=mesh,
        in_specs=placed,
        out_specs=(P("expert", None), P("expert", None, "dp"), P("expert", None, "dp")),
        check_vma=False,
    )
```

```python
import functools

import jax
import jax.numpy as jnp
from jax import lax
from jax.experimental import pallas as pl
from jax.experimental.pallas import tpu as pltpu
from jax.sharding import PartitionSpec as P

MESH = pl.DeviceIdType.MESH
BF16, F32 = jnp.bfloat16, jnp.float32
EXPERTS = 8
NX, NY, NZ = 4, 4, 8
TOK, D, U = 128, 3072, 256
HALF = TOK // 2
XCOLS = D // NX
ZROWS = 16
ZCOLS = XCOLS // 2
FAR_COLS = D // NZ
OWN, UP, DOWN, FAR = 0, 1, 2, 3
TO_Y = ((FAR, 2), (DOWN, 1), (UP, 3))
NEAR = ((DOWN, 1), (UP, 3))
TILE, BACK, TURN = 256, 1536, 512
X_ORDER, Z_ORDER = (2, 1, 3), (4, 3, 5, 2, 6, 1, 7)
NEAR_X, FAR_X = 1, 1


def kernel(
    og_in, routes_in, gates_in, x_in, wg_in, wu_in, wd_in,
    out, gg, gu,
    xo, wgu, wgu_t, wd, g8, dg, ps, pr, s, xr, u, zr, v, yr, yf,
    load_sem, send_sem, recv_sem,
):
    dp, ex = lax.axis_index("dp"), lax.axis_index("expert")
    x, z = lax.rem(dp, NX), lax.div(dp, NX)
    y, c = lax.div(ex, 2), lax.rem(ex, 2)

    def dev(nx, ny, nz, nc):
        return (nz * NX + nx, ny * 2 + nc)

    sib = dev(x, y, z, 1 - c)
    y_at = {d: lax.rem(y + d, NY) for d in (1, 2, 3)}
    x_at = {d: lax.rem(x + d, NX) for d in (1, 2, 3)}
    z_at = {d: lax.rem(z + d, NZ) for d in range(1, NZ)}
    to_y = {d: dev(x, y_at[d], z, c) for d in y_at}
    to_x = {d: dev(x_at[d], y, z, c) for d in x_at}
    to_z = {d: dev(x, y, z_at[d], c) for d in z_at}

    peers = [sib] + list(to_y.values()) + list(to_x.values()) + list(to_z.values())
    barrier = pltpu.get_barrier_semaphore()
    for device in peers:
        pl.semaphore_signal(barrier, inc=1, device_id=device, device_id_type=MESH)

    loads = []

    def load(src, dst):
        assert len(loads) < 8
        copy = pltpu.make_async_copy(src, dst, load_sem.at[len(loads)])
        copy.start()
        loads.append(copy)
        return copy

    sent = []

    def make(src, dst, device, condition=None):
        i = len(sent)
        assert i < N_SEND
        copy = pltpu.make_async_remote_copy(
            src_ref=src, dst_ref=dst, send_sem=send_sem.at[i], recv_sem=recv_sem.at[i],
            device_id=device, device_id_type=MESH,
        )
        sent.append((copy, condition))
        return copy

    def send(src, dst, device):
        copy = make(src, dst, device)
        copy.start()
        return copy

    own_loads = {}
    for h in range(2):
        for a, ref in ((0, x_in), (1, og_in)):
            own_loads[a, h] = load(ref.at[pl.ds(h * HALF, HALF)], xo.at[a, h, OWN, 0])
    weight_loads = [
        load(wg_in.at[0], wgu.at[:, pl.ds(0, U)]),
        load(wu_in.at[0], wgu.at[:, pl.ds(U, U)]),
        load(wd_in.at[0], wd),
    ]

    lane = lax.broadcasted_iota(jnp.int32, (TOK, TOK), 1)
    row = lax.broadcasted_iota(jnp.int32, (TOK, TOK), 0)
    for e in range(EXPERTS):
        g8[OWN, 0, e : e + 1, :] = jnp.sum(
            jnp.where(routes_in[...] == e, gates_in[...], 0.0), axis=0, keepdims=True
        )

    pl.semaphore_wait(barrier, len(peers))
    g_move = {j: send(g8.at[OWN, 0], g8.at[j, 0], to_y[d]) for j, d in TO_Y}
    g_swap = {OWN: send(g8.at[OWN, 0], g8.at[OWN, 1], sib)}

    x_cols = pl.ds(pl.multiple_of(x * XCOLS, XCOLS), XCOLS)
    z_cols = pl.ds(pl.multiple_of(z * FAR_COLS, FAR_COLS), FAR_COLS)

    def groups(first, count):
        return pl.ds(first * 16, count * 16)

    near_x = groups(4 - NEAR_X, NEAR_X)
    far_x, far_z = groups(0, FAR_X), groups(FAR_X, 4 - FAR_X)

    def move(h, j, rows, cols, device):
        piece = xo.at[:, h, OWN, 0, rows, cols]
        return send(piece, xo.at[:, h, j, 0, rows, cols], device)

    swap, swapped = {}, set()

    def do_swap(h, j, first, count):
        rows = groups(first, count)
        copy = send(xo.at[:, h, j, 0, rows], xo.at[:, h, j, 1, rows], sib)
        for g in range(first, first + count):
            swap[h, j, g] = copy

    def swap_wait(h, j, first, count):
        for g in range(first, first + count):
            if id(swap[h, j, g]) not in swapped:
                swapped.add(id(swap[h, j, g]))
                swap[h, j, g].wait_recv()

    def wait_all(copies):
        for copy in copies:
            copy.wait_recv()

    def send_small(h):
        far = []
        if FAR_X < 4:
            far.append(move(h, FAR, far_z, z_cols, to_y[2]))
        if FAR_X:
            far.append(move(h, FAR, far_x, x_cols, to_y[2]))
        near = [move(h, j, near_x, x_cols, to_y[d]) for j, d in NEAR if NEAR_X]
        return far, near

    def send_direct(h, first, count):
        return [move(h, j, groups(first, count), slice(None), to_y[d]) for j, d in NEAR]

    def share(h, small):
        far, near = small
        wait_all(far)
        far_got, near_got = [], []
        for d in Z_ORDER if FAR_X < 4 else ():
            piece = xo.at[:, h, FAR, 0, far_z, z_cols]
            far_got.append(send(piece, piece, to_z[d]))
        for d in X_ORDER:
            if FAR_X:
                piece = xo.at[:, h, FAR, 0, far_x, x_cols]
                far_got.append(send(piece, piece, to_x[d]))
        wait_all(near)
        for d in X_ORDER:
            if NEAR_X:
                piece = xo.at[:, h, pl.ds(UP, 2), 0, near_x, x_cols]
                near_got.append(send(piece, piece, to_x[d]))
        return far_got, near_got

    def far_arrive(h, got):
        wait_all(got)
        do_swap(h, FAR, 0, 4)

    def near_arrive(h, got, first, count):
        wait_all(got)
        for j, _ in NEAR:
            do_swap(h, j, first, count)

    for a in range(2):
        own_loads[a, 0].wait()
    small_0 = send_small(0)
    for a in range(2):
        own_loads[a, 1].wait()
    small_1 = send_small(1)
    first_0 = send_direct(0, 0, 2)
    second_0 = send_direct(0, 2, 2 - NEAR_X)
    do_swap(0, OWN, 0, 4)
    do_swap(1, OWN, 0, 4)

    def weight_column(h, j, slot, first, count):
        mine = lax.broadcasted_iota(jnp.int32, (EXPERTS, TOK), 0) == ex
        line = jnp.sum(jnp.where(mine, g8[j, slot], 0.0), axis=0, keepdims=True)
        whole = jnp.sum(jnp.where(lane == row, line, 0.0), axis=1, keepdims=True)
        start = h * HALF + first * 16
        return whole[start : start + count * 16]

    def compute(h, j, n, first, count):
        rows, sub = n * 2 * count * 16, groups(first, count)
        for jj in range(j, j + n):
            swap_wait(h, jj, first, count)
        weight = jnp.concatenate(
            [weight_column(h, jj, slot, first, count) for jj in range(j, j + n) for slot in range(2)],
            axis=0,
        )
        tokens = xo[0, h, j : j + n, :, sub].reshape(rows, D)
        gate_pre = jnp.dot(tokens, wgu[:, :U], preferred_element_type=F32)
        up_pre = jnp.dot(tokens, wgu[:, U:], preferred_element_type=F32)
        grads_in = xo[1, h, j : j + n, :, sub].reshape(rows, D)
        hidden = weight * jnp.dot(grads_in, wd[...], preferred_element_type=F32)
        sig = jax.nn.sigmoid(gate_pre)
        up_grad = (hidden * (gate_pre * sig)).astype(BF16)
        gate_grad = (hidden * up_pre * sig * (1.0 + gate_pre * (1.0 - sig))).astype(BF16)
        both = jnp.concatenate([gate_grad, up_grad], axis=1)
        dg[h, j : j + n, :, sub] = both.reshape(n, 2, count * 16, 2 * U)

        sends = []
        for i in range(D // BACK):
            cols = pl.ds(i * BACK, BACK)
            part = jnp.dot(both, wgu_t[:, cols], preferred_element_type=F32)
            part = part.astype(BF16).reshape(n, 2, count * 16, BACK)
            ps[h, j : j + n, sub, cols] = part[:, 1]
            piece = (h, pl.ds(j, n), sub, cols)
            sends.append(send(ps.at[piece], pr.at[piece], sib))
            s[h, j : j + n, sub, cols] = part[:, 0]
        return sends

    def merge(h, j, n, first, count, parts):
        sub = groups(first, count)
        wait_all(parts)
        for jj in range(j, j + n):
            s[h, jj, sub] = (s[h, jj, sub].astype(F32) + pr[h, jj, sub].astype(F32)).astype(BF16)

    def send_x(h, j, n, first, count):
        sub = groups(first, count)
        got = []
        for d in X_ORDER:
            cols = pl.ds(pl.multiple_of(x_at[d] * XCOLS, XCOLS), XCOLS)
            got.append(
                send(s.at[h, pl.ds(j, n), sub, cols], xr.at[d - 1, h, pl.ds(j, n), sub], to_x[d])
            )
        return got

    def scatter_x(h, j, n, first, count, parts):
        merge(h, j, n, first, count, parts)
        return send_x(h, j, n, first, count)

    def scatter_near(h, j, n, first, count, parts):
        merge(h, j, n, first, count, parts)
        sub = groups(first, count)
        return [
            send(s.at[h, UP, sub], yf.at[0, sub], to_y[1]),
            send(s.at[h, DOWN, sub], yf.at[1, sub], to_y[3]),
        ]

    def sum_near(h, j, n, first, count, got):
        wait_all(got)
        sub = groups(first, count)
        total = s[h, OWN, sub].astype(F32) + yf[0, sub].astype(F32) + yf[1, sub].astype(F32)
        s[h, OWN, sub] = total.astype(BF16)
        return send_x(h, OWN, 1, first, count)

    y_got = {0: [], 1: []}
    y_dist = {UP: 1, DOWN: 3, FAR: 2}

    def sum_x(h, j, n, first, count, got):
        sub = groups(first, count)
        wait_all(got)
        for jj in range(j, j + n):
            total = s[h, jj, sub, x_cols].astype(F32)
            for d in range(3):
                total = total + xr[d, h, jj, sub].astype(F32)
            u[h, jj, sub] = total.astype(BF16)
            if jj != OWN:
                y_got[h].append(send(u.at[h, jj, sub], yr.at[h, jj - 1, sub], to_y[y_dist[jj]]))

    def z_part(nz):
        rows = pl.ds(pl.multiple_of(lax.rem(nz, 4) * ZROWS, ZROWS), ZROWS)
        return rows, pl.ds(pl.multiple_of(lax.div(nz, 4) * ZCOLS, ZCOLS), ZCOLS)

    def scatter_z(h):
        wait_all(y_got[h])
        total = u[h, OWN].astype(F32)
        for j in range(3):
            total = total + yr[h, j].astype(F32)
        v[h] = total.astype(BF16)
        got = []
        for d in Z_ORDER:
            rows, cols = z_part(z_at[d])
            got.append(send(v.at[h, rows, cols], zr.at[d - 1, h], to_z[d]))
        return got

    def gather_z(h, got):
        wait_all(got)
        rows, cols = z_part(z)
        total = v[h, rows, cols].astype(F32)
        for d in range(NZ - 1):
            total = total + zr[d, h].astype(F32)
        rows = pl.ds(pl.multiple_of(h * HALF + lax.rem(z, 4) * ZROWS, ZROWS), ZROWS)
        cols = pl.ds(pl.multiple_of(x * XCOLS + lax.div(z, 4) * ZCOLS, ZCOLS), ZCOLS)
        out[rows, cols] = total.astype(BF16)
        piece = out.at[rows, cols]
        return [send(piece, piece, to_z[d]) for d in Z_ORDER]

    def owns(nz, part):
        return lax.div(lax.rem(nz, 4), 2) == part

    def scatter_z_part(part):
        if part == 0:
            wait_all(y_got[1])
        sub = groups(2 * part, 2)
        v[1, sub] = (u[1, OWN, sub].astype(F32) + yr[1, FAR - 1, sub].astype(F32)).astype(BF16)
        got = []
        for d in Z_ORDER:
            rows, cols = z_part(z_at[d])
            theirs = owns(z_at[d], part)
            copy = make(v.at[1, rows, cols], zr.at[d - 1, 1], to_z[d], theirs)
            pl.when(theirs)(copy.start)
            got.append(copy)
        return got

    def gather_z_part(part, got):
        rows, cols = z_part(z)
        out_rows = pl.ds(pl.multiple_of(HALF + lax.rem(z, 4) * ZROWS, ZROWS), ZROWS)
        out_cols = pl.ds(pl.multiple_of(x * XCOLS + lax.div(z, 4) * ZCOLS, ZCOLS), ZCOLS)
        piece = out.at[out_rows, out_cols]
        mine = owns(z, part)
        gathered = [(d, make(piece, piece, to_z[d], mine)) for d in Z_ORDER]

        @pl.when(mine)
        def _():
            wait_all(got)
            total = v[1, rows, cols].astype(F32)
            for d in range(NZ - 1):
                total = total + zr[d, 1].astype(F32)
            out[out_rows, out_cols] = total.astype(BF16)
            for _, copy in gathered:
                copy.start()

        return gathered

    def gather_x_part(part, gathered):
        for d, copy in gathered:
            pl.when(owns(lax.rem(z + NZ - d, NZ), part))(copy.wait_recv)
        piece = out.at[pl.ds(HALF + part * 2 * ZROWS, 2 * ZROWS), x_cols]
        return [send(piece, piece, to_x[d]) for d in X_ORDER]

    def gather_x(h, got):
        wait_all(got)
        piece = out.at[pl.ds(h * HALF, HALF), x_cols]
        return [send(piece, piece, to_x[d]) for d in X_ORDER]

    def grad_tiles(first, last):
        def tile(i, carry):
            cols = pl.ds(pl.multiple_of(i * TILE, TILE), TILE)
            part = lax.dot_general(
                xo[0, :, :, :, :, cols].reshape(8 * TOK, TILE),
                dg[...].reshape(8 * TOK, 2 * U),
                (((0,), (0,)), ((), ())),
                preferred_element_type=F32,
            )
            gg[0, cols] = part[:, :U]
            gu[0, cols] = part[:, U:]
            return carry

        lax.fori_loop(first, last, tile, 0)

    own0, own1 = (0, OWN, 1, 0, 4), (1, OWN, 1, 0, 4)
    near0, far0, far1 = (0, UP, 2, 0, 4), (0, FAR, 1, 0, 4), (1, FAR, 1, 0, 4)
    first1, second1 = (1, UP, 2, 0, 2), (1, UP, 2, 2, 2)

    for copy in weight_loads:
        copy.wait()

    def turn(i, carry):
        cols = pl.ds(pl.multiple_of(i * TURN, TURN), TURN)
        wgu_t[:, cols] = wgu[cols, :].T
        return carry

    lax.fori_loop(0, D // TURN, turn, 0)
    g_swap[OWN].wait_recv()
    p_own0 = compute(*own0)
    far_0, shared_0 = share(0, small_0)
    far_1, shared_1 = share(1, small_1)
    first_1 = send_direct(1, 0, 2)
    p_own1 = compute(*own1)
    for j, _ in TO_Y:
        g_move[j].wait_recv()
        g_swap[j] = send(g8.at[j, 0], g8.at[j, 1], sib)
    x_own0 = scatter_x(*own0, p_own0)
    merge(*own1, p_own1)
    near_arrive(0, first_0, 0, 2)
    near_arrive(0, second_0, 2, 2 - NEAR_X)
    second_1 = send_direct(1, 2, 2 - NEAR_X)
    if NEAR_X:
        near_arrive(0, shared_0, 4 - NEAR_X, NEAR_X)
    for j, _ in TO_Y:
        g_swap[j].wait_recv()
    p_near0 = compute(*near0)
    sum_x(*own0, x_own0)
    x_near0 = scatter_x(*near0, p_near0)
    far_arrive(0, far_0)
    p_far0 = compute(*far0)
    near_arrive(1, first_1, 0, 2)
    x_far0 = scatter_x(*far0, p_far0)
    p_first1 = compute(*first1)
    far_arrive(1, far_1)
    y_first1 = scatter_near(*first1, p_first1)
    sum_x(*near0, x_near0)
    p_far1 = compute(*far1)
    near_arrive(1, second_1, 2, 2 - NEAR_X)
    if NEAR_X:
        near_arrive(1, shared_1, 4 - NEAR_X, NEAR_X)
    x_far1 = scatter_x(*far1, p_far1)
    p_second1 = compute(*second1)
    sum_x(*far0, x_far0)
    x_first1 = sum_near(*first1, y_first1)
    y_second1 = scatter_near(*second1, p_second1)
    grad_tiles(0, 4)
    z_0 = scatter_z(0)
    sum_x(*far1, x_far1)
    zg_0 = gather_z(0, z_0)
    sum_x(1, OWN, 1, 0, 2, x_first1)
    x_second1 = sum_near(*second1, y_second1)
    z_first = scatter_z_part(0)
    grad_tiles(4, 8)
    zg_first = gather_z_part(0, z_first)
    sum_x(1, OWN, 1, 2, 2, x_second1)
    z_second = scatter_z_part(1)
    xg_0 = gather_x(0, zg_0)
    grad_tiles(8, 10)
    xg_first = gather_x_part(0, zg_first)
    zg_second = gather_z_part(1, z_second)
    grad_tiles(10, 12)
    xg_second = gather_x_part(1, zg_second)
    wait_all(xg_0 + xg_first + xg_second)
    for copy, condition in sent:
        if condition is None:
            copy.wait_send()
        else:
            pl.when(condition)(copy.wait_send)


N_SEND = 176


def local(out_grad, routes, gate_values, layer_input, w_gate, w_up, w_down):
    any_spec = pl.BlockSpec(memory_space=pl.ANY)
    vmem = pl.BlockSpec(memory_space=pltpu.VMEM)
    return pl.pallas_call(
        kernel,
        out_shape=(
            pltpu.VMEM((TOK, D), BF16),
            pltpu.VMEM((1, D, U), F32),
            pltpu.VMEM((1, D, U), F32),
        ),
        in_specs=[any_spec, vmem, vmem, any_spec, any_spec, any_spec, any_spec],
        out_specs=(vmem, vmem, vmem),
        scratch_shapes=[
            pltpu.VMEM((2, 2, 4, 2, HALF, D), BF16),
            pltpu.VMEM((D, 2 * U), BF16),
            pltpu.VMEM((2 * U, D), BF16),
            pltpu.VMEM((D, U), BF16),
            pltpu.VMEM((4, 2, EXPERTS, TOK), F32),
            pltpu.VMEM((2, 4, 2, HALF, 2 * U), BF16),
            pltpu.VMEM((2, 4, HALF, D), BF16),
            pltpu.VMEM((2, 4, HALF, D), BF16),
            pltpu.VMEM((2, 4, HALF, D), BF16),
            pltpu.VMEM((3, 2, 4, HALF, XCOLS), BF16),
            pltpu.VMEM((2, 4, HALF, XCOLS), BF16),
            pltpu.VMEM((NZ - 1, 2, ZROWS, ZCOLS), BF16),
            pltpu.VMEM((2, HALF, XCOLS), BF16),
            pltpu.VMEM((2, 3, HALF, XCOLS), BF16),
            pltpu.VMEM((2, HALF, D), BF16),
            pltpu.SemaphoreType.DMA((8,)),
            pltpu.SemaphoreType.DMA((N_SEND,)),
            pltpu.SemaphoreType.DMA((N_SEND,)),
        ],
        compiler_params=pltpu.CompilerParams(
            collective_id=0, has_side_effects=True, vmem_limit_bytes=56 * 2**20
        ),
        cost_estimate=pl.CostEstimate(
            flops=7 * 2 * 1024 * D * U, bytes_accessed=14 * 2**20, transcendentals=1024 * U
        ),
    )(out_grad, routes.T, gate_values.T, layer_input, w_gate, w_up, w_down)


def solution(mesh):
    placed = (
        P("expert", None),
        P("expert", None),
        P("expert", None),
        P("expert", None),
        P("expert", None, "dp"),
        P("expert", None, "dp"),
        P("expert", None, "dp"),
    )
    return jax.shard_map(
        local,
        mesh=mesh,
        in_specs=placed,
        out_specs=(P("expert", None), P("expert", None, "dp"), P("expert", None, "dp")),
        check_vma=False,
    )
```
